128 devices in a mesh: blk: 32 (over x, y, core), chain: 4 (over z).
Axes of the slice: x: 4, y: 4, z: 4, core: 2. Of those that a mesh axis runs over, the one named last changes fastest.
Arguments:
- rhs: float32 [4, 2, 32, 256, 256], P('chain', None, 'blk'), may hold values from -6 to 6
- inverses: bfloat16 [4, 2, 32, 256, 256], P('chain', None, 'blk'), as said below
- blocks: bfloat16 [4, 2, 32, 8, 256, 256], P('chain', None, 'blk'), may hold values from -0.125 to 0.125
- pattern: int32 [4, 2, 32, 8], P('chain', None, 'blk'), may hold values from 0 to 63
Outputs:
- forward_solution: float32 [4, 2, 32, 256, 256], P('chain', None, 'blk')
- solution: float32 [4, 2, 32, 256, 256], P('chain', None, 'blk')
The draws below stay inside these ranges and needn't reach their ends.
Inputs may be any that keep to these rules, and one draw needn't show every extreme that they name: `pattern`: every entry names a supernode of the next level. `inverses`: each block is the identity plus entries of standard deviation about 0.5 / sqrt(256).
All inputs are finite; a program needn't handle non-finite values.
Results may differ from the reference program's by a relative error of at most 0.025.
Values may be sent and summed in bfloat16 or wider, within the bound.
No kernel may reach another device: no remote copies, remote signals or barrier semaphores. Data moves between devices by JAX's collectives and lax.ppermute only.
A program may use at most 128 MiB of HBM per device.

```python
import jax
import jax.numpy as jnp
from jax import lax

B = 256
R = 256
P_SIZE = 8
S_DEV = 2
LEVELS = 4
NS = 64
N_BLK = 32


def draw_inverses(key, part):
    key = jax.random.fold_in(key, 7)
    shape = (LEVELS, S_DEV, N_BLK, B, B)
    spread = 0.5 * jax.random.normal(key, shape, jnp.float32) / jnp.sqrt(jnp.float32(B))
    return (spread + jnp.eye(B, dtype=jnp.float32)).astype(jnp.bfloat16)


def place_ends(array, key, least, top_value):
    longest = array.shape.index(max(array.shape))
    spots = []
    for shift in (0, 1):
        where = [jax.random.randint(jax.random.fold_in(key, axis), (), 0, length) for axis, length in enumerate(array.shape)]
        where[longest] = (where[longest] + shift) % array.shape[longest]
        spots.append(tuple(where))
    return array.at[spots[0]].set(least).at[spots[1]].set(top_value)


def steps_of(own_key, dims, cuts, smallest, top_value):
    loudness = 1.0
    for axis_at, parts in cuts:
        steps = jax.random.uniform(jax.random.fold_in(jax.random.fold_in(own_key, 6), axis_at), (parts,), jnp.float32, smallest / len(cuts), top_value / len(cuts))
        loudness = loudness * jnp.repeat(jnp.exp(steps), dims[axis_at] // parts).reshape((-1,) + (1,) * (len(dims) - 1 - axis_at))
    return loudness


def normal_values(own_key, extent, scale, bound, cuts=(), held_as=jnp.bfloat16):
    level = steps_of(own_key, extent, cuts, -0.22, 0.18) if cuts else 1.0
    array = jax.random.normal(own_key, extent, jnp.float32) * scale * level
    return jnp.minimum(jnp.maximum(array, -bound), bound).astype(held_as)


def setup_inputs(seed: int = 0) -> dict:
    key_of = jax.random.split(jax.random.key(seed), 5)
    return {
        "rhs": normal_values(key_of[0], (LEVELS, S_DEV, N_BLK, B, R), 1.0, 6.0, ((0, 4), (2, 32)), jnp.float32),
        "inverses": draw_inverses(jax.random.fold_in(key_of[4], 71), 0),
        "blocks": normal_values(key_of[2], (LEVELS, S_DEV, N_BLK, P_SIZE, B, B), (B * P_SIZE) ** -0.5, 0.125, ((0, 4), (2, 32))),
        "pattern": place_ends(jax.random.randint(key_of[3], (LEVELS, S_DEV, N_BLK, P_SIZE), 0, NS), jax.random.fold_in(key_of[3], 1), 0, NS - 1).astype(jnp.int32),
    }


def fan_in(contrib, targets):
    nodes = jnp.arange(NS, dtype=jnp.int32)

    def owner_step(total, items):
        piece, where = items
        onehot = (where.reshape(-1)[:, None] == nodes[None, :]).astype(jnp.float32)
        share = jnp.dot(onehot.T, piece.reshape(S_DEV * P_SIZE, B * R), precision=lax.Precision.HIGHEST)
        share = lax.optimization_barrier(share.astype(jnp.bfloat16))
        return total + share.astype(jnp.float32), None

    pieces = jnp.transpose(contrib.reshape(S_DEV, N_BLK, P_SIZE, B * R), (1, 0, 2, 3))
    wheres = jnp.transpose(targets.reshape(S_DEV, N_BLK, P_SIZE), (1, 0, 2))
    total, _ = lax.scan(owner_step, jnp.zeros((NS, B * R), jnp.float32), (pieces, wheres))
    return total.reshape(NS, B, R)


def reference(rhs, inverses, blocks, pattern):
    right = rhs.reshape(LEVELS, NS, B, R)
    inv = inverses.reshape(LEVELS, NS, B, B).astype(jnp.float32)
    factor = blocks.reshape(LEVELS, NS, P_SIZE, B, B)
    targets = pattern.reshape(LEVELS, NS, P_SIZE)
    inflow = jnp.zeros((NS, B, R), jnp.float32)
    forward_list = []
    for level in range(LEVELS):
        resid = (right[level] - inflow).astype(jnp.bfloat16).astype(jnp.float32)
        forward = jnp.einsum("sij,sjr->sir", inv[level], resid)
        forward_list.append(forward)
        if level < LEVELS - 1:
            solved = forward.astype(jnp.bfloat16).astype(jnp.float32)
            contrib = jnp.einsum("spij,sjr->spir", factor[level].astype(jnp.float32), solved)
            inflow = fan_in(contrib, targets[level])
    solution_list = [None] * LEVELS
    above = None
    for level in reversed(range(LEVELS)):
        if level == LEVELS - 1:
            upper = forward_list[level]
        else:
            parents = above.astype(jnp.bfloat16).astype(jnp.float32)
            picked = parents[targets[level]]
            back = jnp.einsum("spji,spjr->sir", factor[level].astype(jnp.float32), picked)
            upper = forward_list[level] - back
        upper = upper.astype(jnp.bfloat16).astype(jnp.float32)
        above = jnp.einsum("sji,sjr->sir", inv[level], upper)
        solution_list[level] = above
    shape = (LEVELS, S_DEV, N_BLK, B, R)
    return jnp.stack(forward_list).reshape(shape), jnp.stack(solution_list).reshape(shape)
```

```python
import functools

import jax
import jax.numpy as jnp
from jax import lax
from jax.experimental import pallas as pl
from jax.experimental.pallas import tpu as pltpu
from jax.sharding import Mesh, PartitionSpec as P


BF = jnp.bfloat16
F32 = jnp.float32
VMEM = 56 * 1024 * 1024
NODES = 64
CHIPS = 16
WIDTH = 256
FAN = 8
HALF = 128
COLS = 32


def dot_t(a, b):
    return lax.dot_general(a, b, (((1,), (1,)), ((), ())), preferred_element_type=F32)


def dot_n(a, b):
    return lax.dot_general(a, b, (((1,), (0,)), ((), ())), preferred_element_type=F32)


def first_kernel(core_ref, rhs_ref, inv_ref, f_ref, solved_ref, rows_ref):
    core = core_ref[0]
    for j in range(2):
        right = rhs_ref[j]
        f = dot_n(inv_ref[j], right.astype(BF))
        f_ref[j] = f
        ft = jnp.transpose(f).astype(BF)
        rt = jnp.transpose(right).astype(BF)
        for half in range(2):
            rel = jnp.bitwise_xor(core, half)
            solved_ref[rel, j] = ft[half * HALF : (half + 1) * HALF]
            for z in range(4):
                at = half * HALF + z * COLS
                rows_ref[rel, z, j] = rt[at : at + COLS]


def first_step(core, rhs, inverse):
    vm = pl.BlockSpec(memory_space=pltpu.VMEM)
    return pl.pallas_call(
        first_kernel,
        out_shape=(
            jax.ShapeDtypeStruct((2, WIDTH, WIDTH), F32),
            jax.ShapeDtypeStruct((2, 2, HALF, WIDTH), BF),
            jax.ShapeDtypeStruct((2, 4, 2, COLS, WIDTH), BF),
        ),
        in_specs=[pl.BlockSpec(memory_space=pltpu.SMEM), vm, vm],
        out_specs=(vm, vm, vm),
        compiler_params=pltpu.CompilerParams(vmem_limit_bytes=VMEM),
        cost_estimate=pl.CostEstimate(flops=2 * 2 * WIDTH**3, bytes_accessed=2 * 2**20, transcendentals=0),
    )(core, rhs, inverse)


def scatter_terms(step, at_ref, solved, own_ref, other_ref, acc_ref):
    def add(block_ref):
        for p in range(FAN):
            t = at_ref[step, p]
            acc_ref[t] += dot_t(solved, block_ref[0, 0, p])

    @pl.when(step < 2)
    def _():
        add(own_ref)

    @pl.when(step >= 2)
    def _():
        add(other_ref)


def zero_kernel(at_ref, solved_ref, own_ref, other_ref, share_ref, acc_ref):
    step = pl.program_id(0)

    @pl.when(step == 0)
    def _():
        acc_ref[...] = jnp.zeros_like(acc_ref)

    scatter_terms(step, at_ref, solved_ref[0], own_ref, other_ref, acc_ref)

    @pl.when(step == 3)
    def _():
        share_ref[...] = acc_ref[...].astype(BF)


def pair_specs(level, fan):
    own = pl.BlockSpec((1, 1, fan, WIDTH, WIDTH), lambda n, *_: (level, jnp.minimum(n, 1), 0, 0, 0))
    other = pl.BlockSpec((1, 1, fan, WIDTH, WIDTH), lambda n, *_: (level, jnp.maximum(n - 2, 0), 0, 0, 0))
    return [own, other]


def zero_level(at, solved, own, other):
    return pl.pallas_call(
        zero_kernel,
        grid_spec=pltpu.PrefetchScalarGridSpec(
            num_scalar_prefetch=1,
            grid=(4,),
            in_specs=[pl.BlockSpec((1, HALF, WIDTH), lambda n, *_: (n, 0, 0))] + pair_specs(0, FAN),
            out_specs=pl.BlockSpec((NODES, HALF, WIDTH), lambda n, *_: (0, 0, 0)),
            scratch_shapes=[pltpu.VMEM((NODES, HALF, WIDTH), F32)],
        ),
        out_shape=jax.ShapeDtypeStruct((NODES, HALF, WIDTH), BF),
        compiler_params=pltpu.CompilerParams(vmem_limit_bytes=VMEM, dimension_semantics=("arbitrary",)),
        cost_estimate=pl.CostEstimate(flops=2 * 32 * HALF * WIDTH**2, bytes_accessed=8 * 2**20, transcendentals=0),
    )(at, solved, own, other)


def solve_node(step, inflow, rhs_ref, own_inv_ref, other_inv_ref):
    resid = (rhs_ref[0].astype(F32) - inflow).astype(BF)
    inv = jnp.where(step < 2, own_inv_ref[0, 0, 0], other_inv_ref[0, 0, 0])
    return dot_t(resid, inv), inv


def forward_kernel(at_ref, got_ref, rhs_ref, own_inv_ref, other_inv_ref, own_ref, other_ref, f_ref, share_ref, acc_ref):
    step = pl.program_id(0)

    @pl.when(step == 0)
    def _():
        acc_ref[...] = jnp.zeros_like(acc_ref)

    inflow = jnp.sum(got_ref[:, 0].astype(F32), axis=0)
    f, _ = solve_node(step, inflow, rhs_ref, own_inv_ref, other_inv_ref)
    f_ref[0] = f
    scatter_terms(step, at_ref, f.astype(BF), own_ref, other_ref, acc_ref)

    @pl.when(step == 3)
    def _():
        share_ref[...] = acc_ref[...].astype(BF)


def got_spec(got):
    return pl.BlockSpec((got.shape[0], 1, COLS, WIDTH), lambda n, *_: (0, n, 0, 0))


NODE = pl.BlockSpec((1, COLS, WIDTH), lambda n, *_: (n, 0, 0))


def forward_level(level, at, got, rhs, own_inv, other_inv, own, other):
    return pl.pallas_call(
        forward_kernel,
        grid_spec=pltpu.PrefetchScalarGridSpec(
            num_scalar_prefetch=1,
            grid=(4,),
            in_specs=[got_spec(got), NODE] + pair_specs(level, 1) + pair_specs(level, FAN),
            out_specs=(NODE, pl.BlockSpec((NODES, COLS, WIDTH), lambda n, *_: (0, 0, 0))),
            scratch_shapes=[pltpu.VMEM((NODES, COLS, WIDTH), F32)],
        ),
        out_shape=(
            jax.ShapeDtypeStruct((4, COLS, WIDTH), F32),
            jax.ShapeDtypeStruct((NODES, COLS, WIDTH), BF),
        ),
        compiler_params=pltpu.CompilerParams(vmem_limit_bytes=VMEM, dimension_semantics=("arbitrary",)),
        cost_estimate=pl.CostEstimate(flops=2 * 36 * COLS * WIDTH**2, bytes_accessed=6 * 2**20, transcendentals=0),
    )(at, got, rhs, own_inv, other_inv, own, other)


def top_kernel(got_ref, rhs_ref, own_inv_ref, other_inv_ref, f_ref, sol_ref, copies_ref):
    step = pl.program_id(0)
    inflow = jnp.sum(got_ref[:, 0].astype(F32), axis=0)
    f, inv = solve_node(step, inflow, rhs_ref, own_inv_ref, other_inv_ref)
    f_ref[0] = f
    sol = dot_n(f.astype(BF), inv).astype(BF)
    sol_ref[0] = sol
    for k in range(CHIPS):
        copies_ref[k, 0] = sol


COPIES = pl.BlockSpec((CHIPS, 1, COLS, WIDTH), lambda n, *_: (0, n, 0, 0))


def top_level(got, rhs, own_inv, other_inv):
    return pl.pallas_call(
        top_kernel,
        grid=(4,),
        in_specs=[got_spec(got), NODE] + pair_specs(3, 1),
        out_specs=(NODE, NODE, COPIES),
        out_shape=(
            jax.ShapeDtypeStruct((4, COLS, WIDTH), F32),
            jax.ShapeDtypeStruct((4, COLS, WIDTH), BF),
            jax.ShapeDtypeStruct((CHIPS, 4, COLS, WIDTH), BF),
        ),
        compiler_params=pltpu.CompilerParams(vmem_limit_bytes=VMEM, dimension_semantics=("arbitrary",)),
        cost_estimate=pl.CostEstimate(flops=2 * 8 * COLS * WIDTH**2, bytes_accessed=3 * 2**20, transcendentals=0),
    )(got, rhs, own_inv, other_inv)


def backward_kernel(copies, at_ref, above_ref, f_ref, own_inv_ref, other_inv_ref, own_ref, other_ref, sol_ref, *rest):
    step = pl.program_id(0)

    def solve(block_ref, inv_ref):
        picked = jnp.concatenate([above_ref[at_ref[step, p]] for p in range(FAN)], axis=1)
        back = dot_n(picked, block_ref[0, 0].reshape(FAN * WIDTH, WIDTH))
        upper = (f_ref[0] - back).astype(BF)
        sol = dot_n(upper, inv_ref[0, 0, 0]).astype(BF)
        sol_ref[0] = sol
        if copies:
            for k in range(CHIPS):
                rest[0][k, 0] = sol

    @pl.when(step < 2)
    def _():
        solve(own_ref, own_inv_ref)

    @pl.when(step >= 2)
    def _():
        solve(other_ref, other_inv_ref)


def backward_level(level, at, above, f, own_inv, other_inv, own, other):
    copies = level > 0
    out_specs = (NODE, COPIES) if copies else (NODE,)
    out_shape = (jax.ShapeDtypeStruct((4, COLS, WIDTH), BF),)
    if copies:
        out_shape += (jax.ShapeDtypeStruct((CHIPS, 4, COLS, WIDTH), BF),)
    return pl.pallas_call(
        functools.partial(backward_kernel, copies),
        grid_spec=pltpu.PrefetchScalarGridSpec(
            num_scalar_prefetch=1,
            grid=(4,),
            in_specs=[pl.BlockSpec((NODES, COLS, WIDTH), lambda n, *_: (0, 0, 0)), NODE]
            + pair_specs(level, 1)
            + pair_specs(level, FAN),
            out_specs=out_specs,
        ),
        out_shape=out_shape,
        compiler_params=pltpu.CompilerParams(vmem_limit_bytes=VMEM, dimension_semantics=("arbitrary",)),
        cost_estimate=pl.CostEstimate(flops=2 * 36 * COLS * WIDTH**2, bytes_accessed=6 * 2**20, transcendentals=0),
    )(at, above, f, own_inv, other_inv, own, other)


def last_kernel(core_ref, plane_ref, first_ref, f_ref, x_ref, forward_ref, result_ref):
    core = core_ref[0]

    def gather(ref, j):
        halves = []
        for half in range(2):
            rel = jnp.bitwise_xor(core, half)
            halves += [ref[z, rel, j] for z in range(4)]
        return jnp.transpose(jnp.concatenate(halves, axis=0).astype(F32))

    for j in range(2):
        result_ref[j] = gather(x_ref, j)

    @pl.when(plane_ref[0] == 0)
    def _():
        forward_ref[...] = first_ref[...]

    @pl.when(plane_ref[0] != 0)
    def _():
        for j in range(2):
            forward_ref[j] = gather(f_ref, j)


def last_step(core, plane, first, f, x):
    vm = pl.BlockSpec(memory_space=pltpu.VMEM)
    sm = pl.BlockSpec(memory_space=pltpu.SMEM)
    return pl.pallas_call(
        last_kernel,
        out_shape=(jax.ShapeDtypeStruct((2, WIDTH, WIDTH), F32),) * 2,
        in_specs=[sm, sm, vm, vm, vm],
        out_specs=(vm, vm),
        compiler_params=pltpu.CompilerParams(vmem_limit_bytes=VMEM),
        cost_estimate=pl.CostEstimate(flops=0, bytes_accessed=2 * 2**20, transcendentals=0),
    )(core, plane, first, f, x)


def swap(value):
    return lax.ppermute(value, "c", [(0, 1), (1, 0)])


def on_device(rhs, inverses, blocks, pattern):
    core = lax.axis_index("c").astype(jnp.int32)
    plane = lax.axis_index("z").astype(jnp.int32)
    core1, plane1 = core.reshape(1), plane.reshape(1)
    right = rhs.reshape(2, WIDTH, WIDTH)
    inverse = inverses.reshape(2, WIDTH, WIDTH)
    factor = blocks.reshape(2, FAN, WIDTH, WIDTH)
    targets = jnp.clip(pattern.reshape(2, FAN), 0, NODES - 1)

    with jax.named_scope("patterns"):
        pair = jnp.concatenate([targets, swap(targets)], axis=0)
        place = (pair % 32) // 2 * 4 + jnp.bitwise_xor(pair % 2, core) * 2 + pair // 32
        places = lax.all_gather(place, "z", axis=0)

    with jax.named_scope("factor_everywhere"):
        own = lax.all_gather(factor, "z", axis=0)
        other = swap(own)
        own_inv = lax.all_gather(inverse.reshape(2, 1, WIDTH, WIDTH), "z", axis=0)
        other_inv = swap(own_inv)

    with jax.named_scope("level_0"):
        first, solved, rows = first_step(core1, right, inverse)
        solved_pair = jnp.concatenate([solved[0], swap(solved[1])], axis=0)
        near = swap(factor)
        share = zero_level(place, solved_pair, factor[None], near[None])
        got = lax.all_to_all(share.reshape(CHIPS, 4, HALF, WIDTH), ("x", "y"), 0, 0, tiled=True)
        summed = jnp.sum(got.astype(F32), axis=0).astype(BF)
        parts = [summed[:, z * COLS : (z + 1) * COLS] for z in range(4)]
        inflow = jnp.where(plane == 0, parts[0], jnp.zeros_like(parts[0]))
        for z in range(1, 4):
            inflow = inflow + lax.ppermute(parts[z], "z", [(0, z)])

    with jax.named_scope("rhs_by_columns"):
        both = jnp.stack([rows[0], swap(rows[1])], axis=1)
        right_at = lax.all_to_all(both, "z", 0, 0, tiled=True).reshape(4, 4, COLS, WIDTH)

    got = inflow[None]
    forward = [None] * 4
    for level in (1, 2):
        with jax.named_scope(f"forward_{level}"):
            forward[level], share = forward_level(
                level, places[level], got, right_at[level], own_inv, other_inv, own, other
            )
            got = lax.all_to_all(share.reshape(CHIPS, 4, COLS, WIDTH), ("x", "y"), 0, 0, tiled=True)
    result = [None] * 4
    with jax.named_scope("top"):
        forward[3], result[3], copies = top_level(got, right_at[3], own_inv, other_inv)

    with jax.named_scope("forward_0_by_columns"):
        by_plane = solved.reshape(2, 2, 4, COLS, WIDTH)
        halves = jnp.concatenate([by_plane[0], swap(by_plane[1])], axis=0)
        mine = jnp.where(plane == 0, halves[:, 0], jnp.zeros_like(halves[:, 0]))
        for z in range(1, 4):
            mine = mine + lax.ppermute(halves[:, z], "z", [(0, z)])
        forward[0] = mine.astype(F32)

    for level in (2, 1, 0):
        with jax.named_scope(f"backward_{level}"):
            above = lax.all_to_all(copies, ("x", "y"), 0, 0, tiled=True).reshape(NODES, COLS, WIDTH)
            out = backward_level(
                level, places[level], above, forward[level], own_inv, other_inv, own, other
            )
            result[level] = out[0]
            if level > 0:
                copies = out[1]

    with jax.named_scope("to_planes"):
        forward[0] = jnp.zeros_like(forward[1])
        f = jnp.stack(forward).astype(BF).reshape(4, 2, 2, COLS, WIDTH)
        x = jnp.stack(result).reshape(4, 2, 2, COLS, WIDTH)
        fx = jnp.stack([f, x], axis=1)
        fx = jnp.stack([fx[:, :, 0], swap(fx[:, :, 1])], axis=2)
        fx = lax.all_to_all(fx, "z", 0, 0, tiled=True)
        forward_out, result_out = last_step(core1, plane1, first, fx[:, 0], fx[:, 1])
    shape = (1, 2, 1, WIDTH, WIDTH)
    return forward_out.reshape(shape), result_out.reshape(shape)


def solution(mesh):
    wide = Mesh(mesh.devices.reshape(4, 4, 2, 4), ("x", "y", "c", "z"))
    blk = ("x", "y", "c")
    return jax.shard_map(
        on_device,
        mesh=wide,
        in_specs=(
            P("z", None, blk, None, None),
            P("z", None, blk, None, None),
            P("z", None, blk, None, None, None),
            P("z", None, blk, None),
        ),
        out_specs=(P("z", None, blk, None, None), P("z", None, blk, None, None)),
        check_vma=False,
    )
```

```python
import functools

import jax
import jax.numpy as jnp
from jax import lax
from jax.experimental import pallas as pl
from jax.experimental.pallas import tpu as pltpu
from jax.sharding import Mesh, PartitionSpec as P


BF = jnp.bfloat16
F32 = jnp.float32
VMEM = 56 * 1024 * 1024
NODES = 64
CHIPS = 16
WIDTH = 256
FAN = 8
HALF = 128
COLS = 32
UP_1 = [(0, 1), (1, 2), (2, 3)]
DOWN_1 = [(0, 3), (1, 0), (2, 1)]
UP = [(z, (z + 1) % 4) for z in range(4)]
DOWN = [(z, (z + 3) % 4) for z in range(4)]


def dot_t(a, b):
    return lax.dot_general(a, b, (((1,), (1,)), ((), ())), preferred_element_type=F32)


def dot_n(a, b):
    return lax.dot_general(a, b, (((1,), (0,)), ((), ())), preferred_element_type=F32)


def first_kernel(core_ref, rhs_ref, inv_ref, f_ref, solved_ref, rows_ref):
    core = core_ref[0]
    for j in range(2):
        right = rhs_ref[j]
        f = dot_n(inv_ref[j], right.astype(BF))
        f_ref[j] = f
        ft = jnp.transpose(f).astype(BF)
        rt = jnp.transpose(right).astype(BF)
        for half in range(2):
            rel = jnp.bitwise_xor(core, half)
            solved_ref[rel, j] = ft[half * HALF : (half + 1) * HALF]
            for z in range(4):
                at = half * HALF + z * COLS
                rows_ref[rel, z, j] = rt[at : at + COLS]


def first_step(core, rhs, inverse):
    vm = pl.BlockSpec(memory_space=pltpu.VMEM)
    return pl.pallas_call(
        first_kernel,
        out_shape=(
            jax.ShapeDtypeStruct((2, WIDTH, WIDTH), F32),
            jax.ShapeDtypeStruct((2, 2, HALF, WIDTH), BF),
            jax.ShapeDtypeStruct((2, 4, 2, COLS, WIDTH), BF),
        ),
        in_specs=[pl.BlockSpec(memory_space=pltpu.SMEM), vm, vm],
        out_specs=(vm, vm, vm),
        compiler_params=pltpu.CompilerParams(vmem_limit_bytes=VMEM),
        cost_estimate=pl.CostEstimate(flops=2 * 2 * WIDTH**3, bytes_accessed=2 * 2**20, transcendentals=0),
    )(core, rhs, inverse)


def any_specs(count):
    return [pl.BlockSpec(memory_space=pl.ANY)] * count


SMEM = pl.BlockSpec(memory_space=pltpu.SMEM)
VM = pl.BlockSpec(memory_space=pltpu.VMEM)


def fetch(plane, choices, dst, sem):
    for z, src in enumerate(choices):

        @pl.when(plane == z)
        def _():
            pltpu.make_async_copy(src, dst, sem).start()

    return pltpu.make_async_copy(choices[0], dst, sem)


def factor_copies(plane, refs, buf, sems):
    return [fetch(plane, refs[4 * n : 4 * n + 4], buf.at[n], sems.at[n]) for n in range(4)]


def add_terms(n, at_ref, solved, buf, acc_ref):
    rows = buf.shape[1] * WIDTH
    terms = dot_t(solved, buf[n].reshape(rows, WIDTH))
    for p in range(FAN):
        acc_ref[at_ref[n, p]] += terms[:, p * WIDTH : (p + 1) * WIDTH]


def zero_kernel(at_ref, solved_ref, own_ref, other_ref, share_ref, buf, sems, acc_ref):
    copies = []
    for n in range(4):
        src = (own_ref if n < 2 else other_ref).at[n % 2]
        copies.append(pltpu.make_async_copy(src, buf.at[n], sems.at[n]))
        copies[n].start()
    acc_ref[...] = jnp.zeros_like(acc_ref)
    for n in range(4):
        copies[n].wait()
        add_terms(n, at_ref, solved_ref[n], buf, acc_ref)
    share_ref[...] = acc_ref[...].astype(BF)


def zero_level(at, solved, own, other):
    return pl.pallas_call(
        zero_kernel,
        in_specs=[SMEM, VM] + any_specs(2),
        out_specs=VM,
        scratch_shapes=[
            pltpu.VMEM((4, FAN, WIDTH, WIDTH), BF),
            pltpu.SemaphoreType.DMA((4,)),
            pltpu.VMEM((NODES, HALF, WIDTH), F32),
        ],
        out_shape=jax.ShapeDtypeStruct((NODES, HALF, WIDTH), BF),
        compiler_params=pltpu.CompilerParams(vmem_limit_bytes=VMEM),
        cost_estimate=pl.CostEstimate(flops=2 * 32 * HALF * WIDTH**2, bytes_accessed=8 * 2**20, transcendentals=0),
    )(at, solved, own, other)


def solve_node(n, got_ref, rhs_ref, inv_ref):
    inflow = jnp.sum(got_ref[:, n].astype(F32), axis=0)
    resid = (rhs_ref[n].astype(F32) - inflow).astype(BF)
    return dot_t(resid, inv_ref[n])


def forward_kernel(plane_ref, at_ref, got_ref, rhs_ref, inv_ref, *rest):
    refs, (f_ref, share_ref, buf, sems, acc_ref) = rest[:16], rest[16:]
    copies = factor_copies(plane_ref[0], refs, buf, sems)
    acc_ref[...] = jnp.zeros_like(acc_ref)
    for n in range(4):
        f = solve_node(n, got_ref, rhs_ref, inv_ref)
        f_ref[n] = f
        copies[n].wait()
        add_terms(n, at_ref, f.astype(BF), buf, acc_ref)
    share_ref[...] = acc_ref[...].astype(BF)


def forward_level(plane, at, got, rhs, inv, choices):
    return pl.pallas_call(
        forward_kernel,
        in_specs=[SMEM, SMEM, VM, VM, VM] + any_specs(16),
        out_specs=(VM, VM),
        scratch_shapes=[
            pltpu.VMEM((4, FAN, WIDTH, WIDTH), BF),
            pltpu.SemaphoreType.DMA((4,)),
            pltpu.VMEM((NODES, COLS, WIDTH), F32),
        ],
        out_shape=(
            jax.ShapeDtypeStruct((4, COLS, WIDTH), F32),
            jax.ShapeDtypeStruct((NODES, COLS, WIDTH), BF),
        ),
        compiler_params=pltpu.CompilerParams(vmem_limit_bytes=VMEM),
        cost_estimate=pl.CostEstimate(flops=2 * 36 * COLS * WIDTH**2, bytes_accessed=6 * 2**20, transcendentals=0),
    )(plane, at, got, rhs, inv, *choices)


def top_kernel(got_ref, rhs_ref, inv_ref, f_ref, sol_ref, copies_ref):
    for n in range(4):
        f = solve_node(n, got_ref, rhs_ref, inv_ref)
        f_ref[n] = f
        sol = dot_n(f.astype(BF), inv_ref[n]).astype(BF)
        sol_ref[n] = sol
        for k in range(CHIPS):
            copies_ref[k, n] = sol


def top_level(got, rhs, inv):
    return pl.pallas_call(
        top_kernel,
        in_specs=[VM] * 3,
        out_specs=(VM, VM, VM),
        out_shape=(
            jax.ShapeDtypeStruct((4, COLS, WIDTH), F32),
            jax.ShapeDtypeStruct((4, COLS, WIDTH), BF),
            jax.ShapeDtypeStruct((CHIPS, 4, COLS, WIDTH), BF),
        ),
        compiler_params=pltpu.CompilerParams(vmem_limit_bytes=VMEM),
        cost_estimate=pl.CostEstimate(flops=2 * 8 * COLS * WIDTH**2, bytes_accessed=3 * 2**20, transcendentals=0),
    )(got, rhs, inv)


def backward_kernel(plane_ref, at_ref, above_ref, f_ref, inv_ref, *rest):
    refs, outs, (buf, sems) = rest[:16], rest[16:-2], rest[-2:]
    copies = factor_copies(plane_ref[0], refs, buf, sems)
    for n in range(4):
        picked = jnp.concatenate([above_ref[at_ref[n, p]] for p in range(FAN)], axis=1)
        copies[n].wait()
        back = dot_n(picked, buf[n].reshape(FAN * WIDTH, WIDTH))
        upper = (f_ref[n] - back).astype(BF)
        sol = dot_n(upper, inv_ref[n]).astype(BF)
        outs[0][n] = sol
        if len(outs) > 1:
            for k in range(CHIPS):
                outs[1][k, n] = sol


def backward_level(level, plane, at, above, f, inv, choices):
    out_shape = (jax.ShapeDtypeStruct((4, COLS, WIDTH), BF),)
    if level > 0:
        out_shape += (jax.ShapeDtypeStruct((CHIPS, 4, COLS, WIDTH), BF),)
    return pl.pallas_call(
        backward_kernel,
        in_specs=[SMEM, SMEM, VM, VM, VM] + any_specs(16),
        out_specs=(VM,) * len(out_shape),
        scratch_shapes=[
            pltpu.VMEM((4, FAN, WIDTH, WIDTH), BF),
            pltpu.SemaphoreType.DMA((4,)),
        ],
        out_shape=out_shape,
        compiler_params=pltpu.CompilerParams(vmem_limit_bytes=VMEM),
        cost_estimate=pl.CostEstimate(flops=2 * 36 * COLS * WIDTH**2, bytes_accessed=6 * 2**20, transcendentals=0),
    )(plane, at, above, f, inv, *choices)


def last_kernel(core_ref, plane_ref, first_ref, f_ref, x_ref, forward_ref, result_ref):
    core = core_ref[0]

    def gather(ref, j):
        halves = []
        for half in range(2):
            rel = jnp.bitwise_xor(core, half)
            halves += [ref[z, rel, j] for z in range(4)]
        return jnp.transpose(jnp.concatenate(halves, axis=0).astype(F32))

    for j in range(2):
        result_ref[j] = gather(x_ref, j)

    @pl.when(plane_ref[0] == 0)
    def _():
        forward_ref[...] = first_ref[...]

    @pl.when(plane_ref[0] != 0)
    def _():
        for j in range(2):
            forward_ref[j] = gather(f_ref, j)


def last_step(core, plane, first, f, x):
    vm = pl.BlockSpec(memory_space=pltpu.VMEM)
    sm = pl.BlockSpec(memory_space=pltpu.SMEM)
    return pl.pallas_call(
        last_kernel,
        out_shape=(jax.ShapeDtypeStruct((2, WIDTH, WIDTH), F32),) * 2,
        in_specs=[sm, sm, vm, vm, vm],
        out_specs=(vm, vm),
        compiler_params=pltpu.CompilerParams(vmem_limit_bytes=VMEM),
        cost_estimate=pl.CostEstimate(flops=0, bytes_accessed=2 * 2**20, transcendentals=0),
    )(core, plane, first, f, x)


def swap(value):
    return lax.ppermute(value, "c", [(0, 1), (1, 0)])


def on_device(rhs, inverses, blocks, pattern):
    core = lax.axis_index("c").astype(jnp.int32)
    plane = lax.axis_index("z").astype(jnp.int32)
    core1, plane1 = core.reshape(1), plane.reshape(1)
    right = rhs.reshape(2, WIDTH, WIDTH)
    inverse = inverses.reshape(2, WIDTH, WIDTH)
    factor = blocks.reshape(2, FAN, WIDTH, WIDTH)
    targets = jnp.clip(pattern.reshape(2, FAN), 0, NODES - 1)

    def places_of(pair):
        return (pair % 32) // 2 * 4 + jnp.bitwise_xor(pair % 2, core) * 2 + pair // 32

    with jax.named_scope("factor_step_1"):
        own_a, own_b = factor[0], factor[1]
        up_1 = lax.ppermute(own_a, "z", UP_1)
        down_1 = lax.ppermute(own_b, "z", DOWN_1)
        near = swap(factor)

    with jax.named_scope("inverses_and_patterns"):
        tail = jnp.pad(targets.astype(BF)[:, None], ((0, 0), (0, 15), (0, WIDTH - FAN)))
        small = lax.all_gather(jnp.concatenate([inverse, tail], axis=1), "z", axis=0)
        small = jnp.concatenate([small, swap(small)], axis=1)
        inv_at = small[:, :, :WIDTH]
        places = places_of(small[:, :, WIDTH, :FAN].astype(jnp.int32))

    with jax.named_scope("level_0"):
        first, solved, rows = first_step(core1, right, inverse)
        solved_pair = jnp.concatenate([solved[0], swap(solved[1])], axis=0)
        place = places_of(jnp.concatenate([targets, swap(targets)], axis=0))
        share = zero_level(place, solved_pair, factor, near)
        got = lax.all_to_all(share.reshape(CHIPS, 4, HALF, WIDTH), ("x", "y"), 0, 0, tiled=True)

    with jax.named_scope("factor_step_2"):
        up_2 = lax.ppermute(jnp.where(plane <= 1, own_b, up_1), "z", UP)
        down_2 = lax.ppermute(jnp.where((plane == 1) | (plane == 2), own_a, down_1), "z", DOWN)
        up_1o, down_1o = swap(up_1), swap(down_1)
    with jax.named_scope("factor_step_3"):
        up_3 = lax.ppermute(jnp.where(plane == 1, up_1, own_b), "z", [(1, 2), (2, 3)])
        down_3 = lax.ppermute(jnp.where(plane == 0, own_a, down_1), "z", [(0, 3), (1, 0)])
        up_2o, down_2o = swap(up_2), swap(down_2)
        up_3o, down_3o = swap(up_3), swap(down_3)

    def choices_of(a, b, u1, d1, u2, d2, u3, d3):
        return {
            0: ([a, u1, u3, d3], [b, u2, d2, d1]),
            1: ([d2, a, u1, u2], [d1, b, u2, d2]),
            2: ([u2, d2, a, u1], [d3, d1, b, u3]),
        }

    mine = choices_of(own_a, own_b, up_1, down_1, up_2, down_2, up_3, down_3)
    theirs = choices_of(near[0], near[1], up_1o, down_1o, up_2o, down_2o, up_3o, down_3o)
    choices = {k: mine[k][0] + mine[k][1] + theirs[k][0] + theirs[k][1] for k in mine}

    with jax.named_scope("level_0_to_columns"):
        summed = jnp.sum(got.astype(F32), axis=0).astype(BF)
        parts = [summed[:, z * COLS : (z + 1) * COLS] for z in range(4)]
        inflow = jnp.where(plane == 0, parts[0], jnp.zeros_like(parts[0]))
        for z in range(1, 4):
            inflow = inflow + lax.ppermute(parts[z], "z", [(0, z)])

    with jax.named_scope("rhs_by_columns"):
        both = jnp.stack([rows[0], swap(rows[1])], axis=1)
        right_at = lax.all_to_all(both, "z", 0, 0, tiled=True).reshape(4, 4, COLS, WIDTH)

    got = inflow[None]
    forward = [None] * 4
    for level in (1, 2):
        with jax.named_scope(f"forward_{level}"):
            forward[level], share = forward_level(
                plane1, places[level], got, right_at[level], inv_at[level], choices[level]
            )
            got = lax.all_to_all(share.reshape(CHIPS, 4, COLS, WIDTH), ("x", "y"), 0, 0, tiled=True)
    result = [None] * 4
    with jax.named_scope("top"):
        forward[3], result[3], copies = top_level(got, right_at[3], inv_at[3])

    with jax.named_scope("forward_0_by_columns"):
        by_plane = solved.reshape(2, 2, 4, COLS, WIDTH)
        halves = jnp.concatenate([by_plane[0], swap(by_plane[1])], axis=0)
        mine = jnp.where(plane == 0, halves[:, 0], jnp.zeros_like(halves[:, 0]))
        for z in range(1, 4):
            mine = mine + lax.ppermute(halves[:, z], "z", [(0, z)])
        forward[0] = mine.astype(F32)

    for level in (2, 1, 0):
        with jax.named_scope(f"backward_{level}"):
            above = lax.all_to_all(copies, ("x", "y"), 0, 0, tiled=True).reshape(NODES, COLS, WIDTH)
            out = backward_level(
                level, plane1, places[level], above, forward[level], inv_at[level], choices[level]
            )
            result[level] = out[0]
            if level > 0:
                copies = out[1]

    with jax.named_scope("to_planes"):
        forward[0] = jnp.zeros_like(forward[1])
        f = jnp.stack(forward).astype(BF).reshape(4, 2, 2, COLS, WIDTH)
        x = jnp.stack(result).reshape(4, 2, 2, COLS, WIDTH)
        fx = jnp.stack([f, x], axis=1)
        fx = jnp.stack([fx[:, :, 0], swap(fx[:, :, 1])], axis=2)
        fx = lax.all_to_all(fx, "z", 0, 0, tiled=True)
        forward_out, result_out = last_step(core1, plane1, first, fx[:, 0], fx[:, 1])
    shape = (1, 2, 1, WIDTH, WIDTH)
    return forward_out.reshape(shape), result_out.reshape(shape)


def solution(mesh):
    wide = Mesh(mesh.devices.reshape(4, 4, 2, 4), ("x", "y", "c", "z"))
    blk = ("x", "y", "c")
    return jax.shard_map(
        on_device,
        mesh=wide,
        in_specs=(
            P("z", None, blk, None, None),
            P("z", None, blk, None, None),
            P("z", None, blk, None, None, None),
            P("z", None, blk, None),
        ),
        out_specs=(P("z", None, blk, None, None), P("z", None, blk, None, None)),
        check_vma=False,
    )
```

```python
import functools

import jax
import jax.numpy as jnp
from jax import lax
from jax.experimental import pallas as pl
from jax.experimental.pallas import tpu as pltpu
from jax.sharding import Mesh, PartitionSpec as P


BF = jnp.bfloat16
F32 = jnp.float32
MIB = 1024 * 1024
LIMIT = 14 * MIB
NODES = 64
CHIPS = 16
WIDTH = 256
FAN = 8
HALF = 128
COLS = 32
UP_1 = [(0, 1), (1, 2), (2, 3)]
DOWN_1 = [(0, 3), (1, 0), (2, 1)]
UP = [(z, (z + 1) % 4) for z in range(4)]
DOWN = [(z, (z + 3) % 4) for z in range(4)]


SMEM = pl.BlockSpec(memory_space=pltpu.SMEM)
VM = pl.BlockSpec(memory_space=pltpu.VMEM)


def dot_t(a, b):
    return lax.dot_general(a, b, (((1,), (1,)), ((), ())), preferred_element_type=F32)


def dot_n(a, b):
    return lax.dot_general(a, b, (((1,), (0,)), ((), ())), preferred_element_type=F32)


KEEP, SEND, INV, PAT, ROWS = 0, 64, 128, 640, 656


def pack_kernel(core_ref, rhs_ref, inv_ref, pat_ref, out_ref):
    core = core_ref[0]
    for z in range(4):
        for j in range(2):
            out_ref[z, INV + j * WIDTH : INV + (j + 1) * WIDTH] = inv_ref[j]
        out_ref[z, PAT:ROWS] = pat_ref[...]
    for j in range(2):
        rt = jnp.transpose(rhs_ref[j]).astype(BF)
        for half in range(2):
            at = pl.multiple_of(jnp.where(core == half, KEEP, SEND) + j * COLS, COLS)
            for z in range(4):
                first = half * HALF + z * COLS
                out_ref[z, pl.ds(at, COLS)] = rt[first : first + COLS]


def pack(core, rhs, inverse, pat):
    return pl.pallas_call(
        pack_kernel,
        out_shape=jax.ShapeDtypeStruct((4, ROWS, WIDTH), BF),
        in_specs=[SMEM, VM, VM, VM],
        out_specs=VM,
        compiler_params=pltpu.CompilerParams(vmem_limit_bytes=8 * MIB),
        cost_estimate=pl.CostEstimate(flops=0, bytes_accessed=2 * 2**20, transcendentals=0),
    )(core, rhs, inverse, pat)


def any_specs(count):
    return [pl.BlockSpec(memory_space=pl.ANY)] * count


def fetch(plane, choices, dst, sem):
    choices = [ref if at is None else ref.at[at] for ref, at in choices]
    for z, src in enumerate(choices):

        @pl.when(plane == z)
        def _():
            pltpu.make_async_copy(src, dst, sem).start()

    return pltpu.make_async_copy(choices[0], dst, sem)


A, B = "A", "B"
WHERE = {
    0: ([A, 0, 2, 3], [B, 2, 3, 1]),
    1: ([3, A, 0, 2], [1, B, 4, 5]),
    2: ([2, 3, A, 0], [5, 1, B, 4]),
}


def factor_copies(level, plane, refs, buf, sems):
    copies = []
    for n in range(4):
        base = refs[7 * (n // 2) : 7 * (n // 2) + 7]
        choices = [(base[0], "AB".index(k)) if k in (A, B) else (base[1 + k], None) for k in WHERE[level][n % 2]]
        copies.append(fetch(plane, choices, buf.at[n], sems.at[n]))
    return copies


def add_terms(n, at_ref, solved, buf, acc_ref):
    rows = buf.shape[1] * WIDTH
    terms = dot_t(solved, buf[n].reshape(rows, WIDTH))
    for p in range(FAN):
        acc_ref[at_ref[n, p]] += terms[:, p * WIDTH : (p + 1) * WIDTH]


def message_copies(level, refs, bufs, sems, parts):
    copies = []
    for r in range(2):
        for k in parts:
            at, size = ((KEEP, SEND)[r], 2 * COLS) if k == 0 else (INV, 2 * WIDTH)
            src = refs[r].at[level, pl.ds(at, size)]
            copies.append(pltpu.make_async_copy(src, bufs[k].at[pl.ds(r * size, size)], sems.at[r, k]))
            copies[-1].start()
    return copies


def rows_of(buf, n, size):
    return buf[n * size : (n + 1) * size]


def forward_kernel(level, plane_ref, at_ref, *rest):
    gots, rest = (rest[:1], rest[1:]) if level else ((), rest)
    told, refs, (f_ref, fb_ref, share_ref, rows, inv, msems, buf, sems, acc_ref) = rest[:2], rest[2:16], rest[16:]
    copies_m = message_copies(level, told, (rows, inv), msems, (0, 1))
    copies = factor_copies(level, plane_ref[0], refs, buf, sems)
    acc_ref[...] = jnp.zeros_like(acc_ref)
    for copy in copies_m:
        copy.wait()
    for n in range(4):
        resid = rows_of(rows, n, COLS)
        if level:
            resid = (resid.astype(F32) - jnp.sum(gots[0][:, n].astype(F32), axis=0)).astype(BF)
        f = dot_t(resid, rows_of(inv, n, WIDTH))
        solved = f.astype(BF)
        f_ref[n] = f
        fb_ref[n] = solved
        copies[n].wait()
        add_terms(n, at_ref, solved, buf, acc_ref)
    share_ref[...] = acc_ref[...].astype(BF)


SMALL = [
    pltpu.VMEM((4 * COLS, WIDTH), BF),
    pltpu.VMEM((4 * WIDTH, WIDTH), BF),
    pltpu.SemaphoreType.DMA((2, 2)),
]
LARGE = [
    pltpu.VMEM((4, FAN, WIDTH, WIDTH), BF),
    pltpu.SemaphoreType.DMA((4,)),
]
NODE_F32 = jax.ShapeDtypeStruct((4, COLS, WIDTH), F32)
NODE_BF = jax.ShapeDtypeStruct((4, COLS, WIDTH), BF)
COPIES = jax.ShapeDtypeStruct((CHIPS, 4, COLS, WIDTH), BF)


def forward_level(level, plane, at, gots, told, factors):
    return pl.pallas_call(
        functools.partial(forward_kernel, level),
        in_specs=[SMEM, SMEM] + [VM] * len(gots) + any_specs(16),
        out_specs=(VM, VM, VM),
        scratch_shapes=SMALL + LARGE + [pltpu.VMEM((NODES, COLS, WIDTH), F32)],
        out_shape=(NODE_F32, NODE_BF, jax.ShapeDtypeStruct((NODES, COLS, WIDTH), BF)),
        compiler_params=pltpu.CompilerParams(vmem_limit_bytes=LIMIT),
        cost_estimate=pl.CostEstimate(flops=2 * 36 * COLS * WIDTH**2, bytes_accessed=6 * 2**20, transcendentals=0),
    )(plane, at, *gots, *told, *factors)


def top_kernel(got_ref, own_told, other_told, fb_ref, sol_ref, copies_ref, rows, inv, msems):
    for copy in message_copies(3, (own_told, other_told), (rows, inv), msems, (0, 1)):
        copy.wait()
    for n in range(4):
        inflow = jnp.sum(got_ref[:, n].astype(F32), axis=0)
        resid = (rows_of(rows, n, COLS).astype(F32) - inflow).astype(BF)
        fb = dot_t(resid, rows_of(inv, n, WIDTH)).astype(BF)
        fb_ref[n] = fb
        sol = dot_n(fb, rows_of(inv, n, WIDTH)).astype(BF)
        sol_ref[n] = sol
        for k in range(CHIPS):
            copies_ref[k, n] = sol


def top_level(got, told):
    return pl.pallas_call(
        top_kernel,
        in_specs=[VM] + any_specs(2),
        out_specs=(VM, VM, VM),
        scratch_shapes=SMALL,
        out_shape=(NODE_BF, NODE_BF, COPIES),
        compiler_params=pltpu.CompilerParams(vmem_limit_bytes=8 * MIB),
        cost_estimate=pl.CostEstimate(flops=2 * 8 * COLS * WIDTH**2, bytes_accessed=3 * 2**20, transcendentals=0),
    )(got, *told)


def backward_kernel(level, plane_ref, at_ref, above_ref, f_ref, *rest):
    told, refs, outs, (rows, inv, msems, buf, sems) = rest[:2], rest[2:16], rest[16:-5], rest[-5:]
    copies_m = message_copies(level, told, (rows, inv), msems, (1,))
    copies = factor_copies(level, plane_ref[0], refs, buf, sems)
    for copy in copies_m:
        copy.wait()
    for n in range(4):
        picked = jnp.concatenate([above_ref[at_ref[n, p]] for p in range(FAN)], axis=1)
        copies[n].wait()
        back = dot_n(picked, buf[n].reshape(FAN * WIDTH, WIDTH))
        upper = (f_ref[n] - back).astype(BF)
        sol = dot_n(upper, rows_of(inv, n, WIDTH)).astype(BF)
        outs[0][n] = sol
        if level:
            for k in range(CHIPS):
                outs[1][k, n] = sol


def backward_level(level, plane, at, above, f, told, factors):
    out_shape = (NODE_BF, COPIES) if level else (NODE_BF,)
    return pl.pallas_call(
        functools.partial(backward_kernel, level),
        in_specs=[SMEM, SMEM, VM, VM] + any_specs(16),
        out_specs=(VM,) * len(out_shape),
        scratch_shapes=SMALL + LARGE,
        out_shape=out_shape,
        compiler_params=pltpu.CompilerParams(vmem_limit_bytes=LIMIT),
        cost_estimate=pl.CostEstimate(flops=2 * 36 * COLS * WIDTH**2, bytes_accessed=6 * 2**20, transcendentals=0),
    )(plane, at, above, f, *told, *factors)


def last_kernel(core_ref, fx_ref, forward_ref, result_ref):
    core = core_ref[0]
    for k, out_ref in enumerate((forward_ref, result_ref)):
        for j in range(2):
            halves = []
            for half in range(2):
                rel = jnp.bitwise_xor(core, half)
                halves += [fx_ref[z, rel, k, j] for z in range(4)]
            out_ref[j] = jnp.transpose(jnp.concatenate(halves, axis=0).astype(F32))


def last_step(core, fx):
    return pl.pallas_call(
        last_kernel,
        out_shape=(jax.ShapeDtypeStruct((2, WIDTH, WIDTH), F32),) * 2,
        in_specs=[SMEM, VM],
        out_specs=(VM, VM),
        compiler_params=pltpu.CompilerParams(vmem_limit_bytes=8 * MIB),
        cost_estimate=pl.CostEstimate(flops=0, bytes_accessed=2 * 2**20, transcendentals=0),
    )(core, fx)


def swap(value):
    return lax.ppermute(value, "c", [(0, 1), (1, 0)])


def exchange(value):
    return lax.all_to_all(value.reshape(CHIPS, 4, COLS, WIDTH), ("x", "y"), 0, 0, tiled=True)


def on_device(rhs, inverses, blocks, pattern):
    core = lax.axis_index("c").astype(jnp.int32)
    plane = lax.axis_index("z").astype(jnp.int32)
    core1, plane1 = core.reshape(1), plane.reshape(1)
    factor = blocks.reshape(2, FAN, WIDTH, WIDTH)

    with jax.named_scope("factor_step_1"):
        own_a, own_b = factor[0], factor[1]
        up_1 = lax.ppermute(own_a, "z", UP_1)
        down_1 = lax.ppermute(own_b, "z", DOWN_1)
        near = swap(factor)

    with jax.named_scope("tell_planes"):
        pat = jnp.pad(pattern.reshape(2, FAN).astype(BF), ((0, ROWS - PAT - 2), (0, WIDTH - FAN)))
        message = pack(core1, rhs.reshape(2, WIDTH, WIDTH), inverses.reshape(2, WIDTH, WIDTH), pat)
        told = lax.all_to_all(message, "z", 0, 0, tiled=True)
        told = (told, swap(told))
        targets = jnp.concatenate([t[:, PAT : PAT + 2, :FAN] for t in told], axis=1).astype(jnp.int32)
        targets = jnp.clip(targets, 0, NODES - 1)
        places = (targets % 32) // 2 * 4 + jnp.bitwise_xor(targets % 2, core) * 2 + targets // 32
        places = [places[k] for k in range(4)]

    with jax.named_scope("factor_step_2"):
        up_2 = lax.ppermute(jnp.where(plane == 0, own_b, up_1), "z", UP)
        down_2 = lax.ppermute(jnp.where(plane == 3, down_1, own_a), "z", DOWN)
        up_1o, down_1o = swap(up_1), swap(down_1)
        up_2, down_2, own_3, down_1 = lax.optimization_barrier((up_2, down_2, own_b, down_1))
        up_2o, down_2o = swap(up_2), swap(down_2)
    with jax.named_scope("factor_step_3"):
        up_3 = lax.ppermute(own_3, "z", [(1, 2), (2, 3)])
        down_3 = lax.ppermute(down_1, "z", [(0, 3), (1, 0)])

    factors = [factor, up_1, down_1, up_2, down_2, factor, factor]
    factors += [near, up_1o, down_1o, up_2o, down_2o, near, near]
    forward = [None] * 3
    solved = [None] * 4
    gots = ()
    for level in range(3):
        with jax.named_scope(f"forward_{level}"):
            forward[level], solved[level], share = forward_level(level, plane1, places[level], gots, told, factors)
            got = exchange(share)
            gots = (got,)
        if level == 0:
            with jax.named_scope("factor_step_3"):
                up_3, down_3, got = lax.optimization_barrier((up_3, down_3, got))
                gots = (got,)
                factors[5:7] = [up_3, down_3]
                factors[12:14] = [swap(up_3), swap(down_3)]
    result = [None] * 4
    with jax.named_scope("top"):
        solved[3], result[3], copies = top_level(got, told)

    for level in (2, 1, 0):
        with jax.named_scope(f"backward_{level}"):
            above = exchange(copies).reshape(NODES, COLS, WIDTH)
            out = backward_level(level, plane1, places[level], above, forward[level], told, factors)
            result[level] = out[0]
            if level > 0:
                copies = out[1]

    with jax.named_scope("to_planes"):
        fx = jnp.stack([jnp.stack(solved), jnp.stack(result)], axis=1).reshape(4, 2, 2, 2, COLS, WIDTH)
        fx = jnp.stack([fx[:, :, 0], swap(fx[:, :, 1])], axis=1)
        fx = lax.all_to_all(fx, "z", 0, 0, tiled=True)
        forward_out, result_out = last_step(core1, fx)
    shape = (1, 2, 1, WIDTH, WIDTH)
    return forward_out.reshape(shape), result_out.reshape(shape)


def solution(mesh):
    wide = Mesh(mesh.devices.reshape(4, 4, 2, 4), ("x", "y", "c", "z"))
    blk = ("x", "y", "c")
    return jax.shard_map(
        on_device,
        mesh=wide,
        in_specs=(
            P("z", None, blk, None, None),
            P("z", None, blk, None, None),
            P("z", None, blk, None, None, None),
            P("z", None, blk, None),
        ),
        out_specs=(P("z", None, blk, None, None), P("z", None, blk, None, None)),
        check_vma=False,
    )
```

```python
import functools

import jax
import jax.numpy as jnp
from jax import lax
from jax.experimental import pallas as pl
from jax.experimental.pallas import tpu as pltpu
from jax.sharding import Mesh, PartitionSpec as P


BF = jnp.bfloat16
F32 = jnp.float32
MIB = 1024 * 1024
LIMIT = 14 * MIB
NODES = 64
CHIPS = 16
WIDTH = 256
FAN = 8
HALF = 128
COLS = 32
UP = [(z, (z + 1) % 4) for z in range(4)]
DOWN = [(z, (z + 3) % 4) for z in range(4)]


SMEM = pl.BlockSpec(memory_space=pltpu.SMEM)
VM = pl.BlockSpec(memory_space=pltpu.VMEM)


def dot_t(a, b):
    return lax.dot_general(a, b, (((1,), (1,)), ((), ())), preferred_element_type=F32)


def dot_n(a, b):
    return lax.dot_general(a, b, (((1,), (0,)), ((), ())), preferred_element_type=F32)


KEEP, SEND, PAT, ROWS = 0, 64, 128, 144


def pack_kernel(core_ref, plane_ref, rhs_ref, pat_ref, out_ref):
    core, plane = core_ref[0], plane_ref[0]
    for k in range(4):
        out_ref[k, PAT:ROWS] = pat_ref[...]
    for j in range(2):
        rt = jnp.transpose(rhs_ref[j]).astype(BF)
        for half in range(2):
            at = pl.multiple_of(jnp.where(core == half, KEEP, SEND) + j * COLS, COLS)
            for z in range(4):
                first = half * HALF + z * COLS
                out_ref[jnp.bitwise_and(z - plane + 4, 3), pl.ds(at, COLS)] = rt[first : first + COLS]


def pack(core, plane, rhs, pat):
    return pl.pallas_call(
        pack_kernel,
        out_shape=jax.ShapeDtypeStruct((4, ROWS, WIDTH), BF),
        in_specs=[SMEM, SMEM, VM, VM],
        out_specs=VM,
        compiler_params=pltpu.CompilerParams(vmem_limit_bytes=8 * MIB),
        cost_estimate=pl.CostEstimate(flops=0, bytes_accessed=2 * MIB, transcendentals=0),
    )(core, plane, rhs, pat)


ANY = pl.BlockSpec(memory_space=pl.ANY)


def any_specs(count):
    return [ANY] * count


PACKED = FAN + 1


def join_kernel(j, blocks_ref, inv_ref, out_ref, sems):
    copies = [pltpu.make_async_copy(inv_ref.at[j], out_ref.at[FAN], sems.at[0])]
    for k in range(4):
        part = pl.ds(2 * k, 2)
        copies.append(pltpu.make_async_copy(blocks_ref.at[j, part], out_ref.at[part], sems.at[1 + k]))
    for copy in copies:
        copy.start()
    for copy in copies:
        copy.wait()


def join(j, blocks, inverse):
    return pl.pallas_call(
        functools.partial(join_kernel, j),
        in_specs=[ANY, ANY],
        out_specs=VM,
        out_shape=jax.ShapeDtypeStruct((PACKED, WIDTH, WIDTH), BF),
        scratch_shapes=[pltpu.SemaphoreType.DMA((5,))],
        compiler_params=pltpu.CompilerParams(vmem_limit_bytes=3 * MIB),
        cost_estimate=pl.CostEstimate(flops=0, bytes_accessed=3 * MIB, transcendentals=0),
    )(blocks, inverse)


def choose_kernel(chosen, plane_ref, here_ref, else_ref, out_ref, sems):
    for k in range(3):
        part = pl.ds(3 * k, 3)

        @pl.when(plane_ref[0] == chosen)
        def _():
            pltpu.make_async_copy(here_ref.at[part], out_ref.at[part], sems.at[k]).start()

        @pl.when(plane_ref[0] != chosen)
        def _():
            pltpu.make_async_copy(else_ref.at[part], out_ref.at[part], sems.at[k]).start()

    for k in range(3):
        part = pl.ds(3 * k, 3)
        pltpu.make_async_copy(else_ref.at[part], out_ref.at[part], sems.at[k]).wait()


def choose(plane, chosen, here, otherwise):
    return pl.pallas_call(
        functools.partial(choose_kernel, chosen),
        in_specs=[SMEM, ANY, ANY],
        out_specs=VM,
        out_shape=jax.ShapeDtypeStruct((PACKED, WIDTH, WIDTH), BF),
        scratch_shapes=[pltpu.SemaphoreType.DMA((3,))],
        compiler_params=pltpu.CompilerParams(vmem_limit_bytes=3 * MIB),
        cost_estimate=pl.CostEstimate(flops=0, bytes_accessed=3 * MIB, transcendentals=0),
    )(plane, here, otherwise)


def fetch(plane, choices, dst, sem):
    for z, src in enumerate(choices):

        @pl.when(plane == z)
        def _():
            pltpu.make_async_copy(src, dst, sem).start()

    return pltpu.make_async_copy(choices[0], dst, sem)


WHERE = {
    0: ([0, 2, 4, 5], [1, 4, 5, 3]),
    1: ([5, 0, 2, 4], [3, 1, 6, 7]),
    2: ([4, 5, 0, 2], [7, 3, 1, 6]),
    3: ([2, 6, 7, 0], [6, 7, 3, 1]),
}


def used(level):
    return sorted(set(WHERE[level][0] + WHERE[level][1]))


def factor_copies(level, plane, refs, buf, sems):
    names = used(level)
    copies = []
    for n in range(4):
        base = refs[len(names) * (n // 2) :]
        choices = [base[names.index(k)] for k in WHERE[level][n % 2]]
        if level == 3:
            choices = [ref.at[FAN] for ref in choices]
        copies.append(fetch(plane, choices, buf.at[n], sems.at[n]))
    return copies


def told_by(plane, level):
    return jnp.bitwise_and(plane - level + 4, 3)


def add_terms(n, at_ref, came, solved, buf, acc_ref):
    terms = dot_t(solved, buf[n, :FAN].reshape(FAN * WIDTH, WIDTH))
    for p in range(FAN):
        acc_ref[at_ref[came, n, p]] += terms[:, p * WIDTH : (p + 1) * WIDTH]


def row_copies(came, refs, rows, sems):
    copies = []
    for r in range(2):
        src = refs[r].at[came, pl.ds((KEEP, SEND)[r], 2 * COLS)]
        copies.append(pltpu.make_async_copy(src, rows.at[pl.ds(2 * COLS * r, 2 * COLS)], sems.at[r]))
        copies[r].start()
    return copies


def rows_of(buf, n, size):
    return buf[n * size : (n + 1) * size]


def inflow_kernel(got_ref, out_ref):
    out_ref[...] = jnp.sum(got_ref[...].astype(F32), axis=0)


def inflow_of(got):
    return pl.pallas_call(
        inflow_kernel,
        in_specs=[VM],
        out_specs=VM,
        out_shape=NODE_F32,
        compiler_params=pltpu.CompilerParams(vmem_limit_bytes=4 * MIB),
        cost_estimate=pl.CostEstimate(flops=MIB, bytes_accessed=MIB, transcendentals=0),
    )(got)


def forward_kernel(level, plane_ref, at_ref, *rest):
    gots, rest = (rest[:1], rest[1:]) if level else ((), rest)
    told, refs, (f_ref, fb_ref, share_ref, rows, rsems, buf, sems, acc_ref) = rest[:2], rest[2:-8], rest[-8:]
    came = told_by(plane_ref[0], level)
    copies_r = row_copies(came, told, rows, rsems)
    copies = factor_copies(level, plane_ref[0], refs, buf, sems)
    acc_ref[...] = jnp.zeros_like(acc_ref)
    for copy in copies_r:
        copy.wait()
    for n in range(4):
        resid = rows_of(rows, n, COLS)
        if level:
            inflow = gots[0][n] if level == 1 else jnp.sum(gots[0][:, n].astype(F32), axis=0)
            resid = (resid.astype(F32) - inflow).astype(BF)
        copies[n].wait()
        f = dot_t(resid, buf[n, FAN])
        solved = f.astype(BF)
        f_ref[n] = f
        fb_ref[n] = solved
        add_terms(n, at_ref, came, solved, buf, acc_ref)
    share_ref[...] = acc_ref[...].astype(BF)


SMALL = [
    pltpu.VMEM((4 * COLS, WIDTH), BF),
    pltpu.SemaphoreType.DMA((2,)),
]
LARGE = [
    pltpu.VMEM((4, PACKED, WIDTH, WIDTH), BF),
    pltpu.SemaphoreType.DMA((4,)),
]
NODE_F32 = jax.ShapeDtypeStruct((4, COLS, WIDTH), F32)
NODE_BF = jax.ShapeDtypeStruct((4, COLS, WIDTH), BF)
COPIES = jax.ShapeDtypeStruct((CHIPS, 4, COLS, WIDTH), BF)


def pick(level, factors):
    return [factors[r][k] for r in range(2) for k in used(level)]


def forward_level(level, plane, at, gots, told, factors):
    blocks = pick(level, factors)
    return pl.pallas_call(
        functools.partial(forward_kernel, level),
        in_specs=[SMEM, SMEM] + [VM] * len(gots) + any_specs(2) + [ANY] * len(blocks),
        out_specs=(VM, VM, VM),
        scratch_shapes=SMALL + LARGE + [pltpu.VMEM((NODES, COLS, WIDTH), F32)],
        out_shape=(NODE_F32, NODE_BF, jax.ShapeDtypeStruct((NODES, COLS, WIDTH), BF)),
        compiler_params=pltpu.CompilerParams(vmem_limit_bytes=LIMIT),
        cost_estimate=pl.CostEstimate(flops=2 * 36 * COLS * WIDTH**2, bytes_accessed=6 * MIB, transcendentals=0),
    )(plane, at, *gots, *told, *blocks)


def top_kernel(plane_ref, got_ref, own_told, other_told, *rest):
    refs, (fb_ref, sol_ref, copies_ref, rows, rsems, invs, sems) = rest[:-7], rest[-7:]
    copies_r = row_copies(told_by(plane_ref[0], 3), (own_told, other_told), rows, rsems)
    copies = factor_copies(3, plane_ref[0], refs, invs, sems)
    for copy in copies_r:
        copy.wait()
    for n in range(4):
        inflow = jnp.sum(got_ref[:, n].astype(F32), axis=0)
        resid = (rows_of(rows, n, COLS).astype(F32) - inflow).astype(BF)
        copies[n].wait()
        inv = invs[n]
        fb = dot_t(resid, inv).astype(BF)
        fb_ref[n] = fb
        sol = dot_n(fb, inv).astype(BF)
        sol_ref[n] = sol
        for k in range(CHIPS):
            copies_ref[k, n] = sol


def top_level(plane, got, told, factors):
    blocks = pick(3, factors)
    return pl.pallas_call(
        top_kernel,
        in_specs=[SMEM, VM] + any_specs(2 + len(blocks)),
        out_specs=(VM, VM, VM),
        scratch_shapes=SMALL + [pltpu.VMEM((4, WIDTH, WIDTH), BF), pltpu.SemaphoreType.DMA((4,))],
        out_shape=(NODE_BF, NODE_BF, COPIES),
        compiler_params=pltpu.CompilerParams(vmem_limit_bytes=8 * MIB),
        cost_estimate=pl.CostEstimate(flops=2 * 8 * COLS * WIDTH**2, bytes_accessed=3 * MIB, transcendentals=0),
    )(plane, got, *told, *blocks)


def backward_kernel(level, plane_ref, at_ref, above_ref, f_ref, *rest):
    count = 2 * len(used(level))
    refs, outs, (buf, sems) = rest[:count], rest[count:-2], rest[-2:]
    copies = factor_copies(level, plane_ref[0], refs, buf, sems)
    came = told_by(plane_ref[0], level)
    for n in range(4):
        picked = jnp.concatenate([above_ref[at_ref[came, n, p]] for p in range(FAN)], axis=1)
        copies[n].wait()
        back = dot_n(picked, buf[n, :FAN].reshape(FAN * WIDTH, WIDTH))
        upper = (f_ref[n] - back).astype(BF)
        sol = dot_n(upper, buf[n, FAN]).astype(BF)
        outs[0][n] = sol
        if level:
            for k in range(CHIPS):
                outs[1][k, n] = sol


def backward_level(level, plane, at, above, f, factors):
    blocks = pick(level, factors)
    out_shape = (NODE_BF, COPIES) if level else (NODE_BF,)
    return pl.pallas_call(
        functools.partial(backward_kernel, level),
        in_specs=[SMEM, SMEM, VM, VM] + any_specs(len(blocks)),
        out_specs=(VM,) * len(out_shape),
        scratch_shapes=LARGE,
        out_shape=out_shape,
        compiler_params=pltpu.CompilerParams(vmem_limit_bytes=LIMIT),
        cost_estimate=pl.CostEstimate(flops=2 * 36 * COLS * WIDTH**2, bytes_accessed=6 * MIB, transcendentals=0),
    )(plane, at, above, f, *blocks)


def last_kernel(core_ref, fx_ref, forward_ref, result_ref):
    core = core_ref[0]
    for k, out_ref in enumerate((forward_ref, result_ref)):
        for j in range(2):
            halves = []
            for half in range(2):
                rel = jnp.bitwise_xor(core, half)
                halves += [fx_ref[z, rel, k, j] for z in range(4)]
            out_ref[j] = jnp.transpose(jnp.concatenate(halves, axis=0).astype(F32))


def last_step(core, fx):
    return pl.pallas_call(
        last_kernel,
        out_shape=(jax.ShapeDtypeStruct((2, WIDTH, WIDTH), F32),) * 2,
        in_specs=[SMEM, VM],
        out_specs=(VM, VM),
        compiler_params=pltpu.CompilerParams(vmem_limit_bytes=8 * MIB),
        cost_estimate=pl.CostEstimate(flops=0, bytes_accessed=2 * 2**20, transcendentals=0),
    )(core, fx)


def swap(value):
    return lax.ppermute(value, "c", [(0, 1), (1, 0)])


def exchange(value):
    return lax.all_to_all(value.reshape(CHIPS, 4, COLS, WIDTH), ("x", "y"), 0, 0, tiled=True)


def on_device(rhs, inverses, blocks, pattern):
    core = lax.axis_index("c").astype(jnp.int32)
    plane = lax.axis_index("z").astype(jnp.int32)
    core1, plane1 = core.reshape(1), plane.reshape(1)
    factor = blocks.reshape(2, FAN, WIDTH, WIDTH)
    inverse = inverses.reshape(2, WIDTH, WIDTH)

    with jax.named_scope("factor_step_1"):
        own_a = join(0, factor, inverse)
        up_1 = lax.ppermute(own_a, "z", UP)
        own_b = join(1, factor, inverse)
        down_1 = lax.ppermute(own_b, "z", DOWN)
        near_a, near_b = swap(own_a), swap(own_b)

    with jax.named_scope("tell_planes"):
        pat = jnp.pad(pattern.reshape(2, FAN).astype(BF), ((0, ROWS - PAT - 2), (0, WIDTH - FAN)))
        message = pack(core1, plane1, rhs.reshape(2, WIDTH, WIDTH), pat)
        told = [message[0]]
        for k in range(1, 4):
            told.append(lax.ppermute(message[k], "z", [(z, (z + k) % 4) for z in range(4)]))
        told = jnp.stack(told)
        up_1, down_1, told = lax.optimization_barrier((up_1, down_1, told))
        told = (told, swap(told))
        targets = jnp.concatenate([t[:, PAT : PAT + 2, :FAN] for t in told], axis=1).astype(jnp.int32)
        targets = jnp.clip(targets, 0, NODES - 1)
        places = (targets % 32) // 2 * 4 + jnp.bitwise_xor(targets % 2, core) * 2 + targets // 32

    with jax.named_scope("factor_step_2"):
        up_2 = lax.ppermute(choose(plane1, 0, own_b, up_1), "z", UP)
        down_2 = lax.ppermute(choose(plane1, 3, down_1, own_a), "z", DOWN)
        up_3 = choose(plane1, 0, up_1, own_b)
        down_3 = choose(plane1, 3, own_a, down_1)
        near = (near_a, near_b, swap(up_1), swap(down_1))
        up_2, down_2, up_3, down_3, told, places, near = lax.optimization_barrier(
            (up_2, down_2, up_3, down_3, told, places, near)
        )
        near += (swap(up_2), swap(down_2))
    with jax.named_scope("factor_step_3"):
        up_3 = lax.ppermute(up_3, "z", UP)
        down_3 = lax.ppermute(down_3, "z", DOWN)

    factors = ([own_a, own_b, up_1, down_1, up_2, down_2], list(near))
    forward = [None] * 3
    solved = [None] * 4
    gots = ()
    for level in range(3):
        with jax.named_scope(f"forward_{level}"):
            forward[level], solved[level], share = forward_level(level, plane1, places, gots, told, factors)
            got = exchange(share)
        if level == 0:
            with jax.named_scope("factor_step_3"):
                up_3, down_3, got = lax.optimization_barrier((up_3, down_3, inflow_of(got)))
                factors[0].extend([up_3, down_3])
                factors[1].extend([swap(up_3), swap(down_3)])
        gots = (got,)
    result = [None] * 4
    with jax.named_scope("top"):
        solved[3], result[3], copies = top_level(plane1, got, told, factors)

    for level in (2, 1, 0):
        with jax.named_scope(f"backward_{level}"):
            above = exchange(copies).reshape(NODES, COLS, WIDTH)
            out = backward_level(level, plane1, places, above, forward[level], factors)
            result[level] = out[0]
            if level > 0:
                copies = out[1]

    with jax.named_scope("to_planes"):
        fx = jnp.stack([jnp.stack(solved), jnp.stack(result)], axis=1).reshape(4, 2, 2, 2, COLS, WIDTH)
        fx = jnp.stack([fx[:, :, 0], swap(fx[:, :, 1])], axis=1)
        fx = lax.all_to_all(fx, "z", 0, 0, tiled=True)
        forward_out, result_out = last_step(core1, fx)
    shape = (1, 2, 1, WIDTH, WIDTH)
    return forward_out.reshape(shape), result_out.reshape(shape)


def solution(mesh):
    wide = Mesh(mesh.devices.reshape(4, 4, 2, 4), ("x", "y", "c", "z"))
    blk = ("x", "y", "c")
    return jax.shard_map(
        on_device,
        mesh=wide,
        in_specs=(
            P("z", None, blk, None, None),
            P("z", None, blk, None, None),
            P("z", None, blk, None, None, None),
            P("z", None, blk, None),
        ),
        out_specs=(P("z", None, blk, None, None), P("z", None, blk, None, None)),
        check_vma=False,
    )
```

```python
import functools

import jax
import jax.numpy as jnp
from jax import lax
from jax.experimental import pallas as pl
from jax.experimental.pallas import tpu as pltpu
from jax.sharding import Mesh, PartitionSpec as P


BF = jnp.bfloat16
F32 = jnp.float32
MIB = 1024 * 1024
LIMIT = 14 * MIB
NODES = 64
CHIPS = 16
WIDTH = 256
FAN = 8
HALF = 128
COLS = 32
UP = [(z, (z + 1) % 4) for z in range(4)]
DOWN = [(z, (z + 3) % 4) for z in range(4)]


SMEM = pl.BlockSpec(memory_space=pltpu.SMEM)
VM = pl.BlockSpec(memory_space=pltpu.VMEM)


def dot_t(a, b):
    return lax.dot_general(a, b, (((1,), (1,)), ((), ())), preferred_element_type=F32)


def dot_n(a, b):
    return lax.dot_general(a, b, (((1,), (0,)), ((), ())), preferred_element_type=F32)


KEEP, SEND, PAT, ROWS = 0, 64, 128, 144


def pack_kernel(core_ref, plane_ref, rhs_ref, pat_ref, out_ref):
    core, plane = core_ref[0], plane_ref[0]
    for k in range(4):
        out_ref[k, PAT:ROWS] = pat_ref[...]
    for j in range(2):
        rt = jnp.transpose(rhs_ref[j]).astype(BF)
        for half in range(2):
            at = pl.multiple_of(jnp.where(core == half, KEEP, SEND) + j * COLS, COLS)
            for z in range(4):
                first = half * HALF + z * COLS
                out_ref[jnp.bitwise_and(z - plane + 4, 3), pl.ds(at, COLS)] = rt[first : first + COLS]


def pack(core, plane, rhs, pat):
    return pl.pallas_call(
        pack_kernel,
        out_shape=jax.ShapeDtypeStruct((4, ROWS, WIDTH), BF),
        in_specs=[SMEM, SMEM, VM, VM],
        out_specs=VM,
        compiler_params=pltpu.CompilerParams(vmem_limit_bytes=8 * MIB),
        cost_estimate=pl.CostEstimate(flops=0, bytes_accessed=2 * MIB, transcendentals=0),
    )(core, plane, rhs, pat)


ANY = pl.BlockSpec(memory_space=pl.ANY)


def any_specs(count):
    return [ANY] * count


PACKED = FAN + 1


def join_kernel(j, blocks_ref, inv_ref, out_ref, sems):
    copies = [pltpu.make_async_copy(inv_ref.at[j], out_ref.at[FAN], sems.at[0])]
    for k in range(4):
        part = pl.ds(2 * k, 2)
        copies.append(pltpu.make_async_copy(blocks_ref.at[j, part], out_ref.at[part], sems.at[1 + k]))
    for copy in copies:
        copy.start()
    for copy in copies:
        copy.wait()


def join(j, blocks, inverse):
    return pl.pallas_call(
        functools.partial(join_kernel, j),
        in_specs=[ANY, ANY],
        out_specs=VM,
        out_shape=jax.ShapeDtypeStruct((PACKED, WIDTH, WIDTH), BF),
        scratch_shapes=[pltpu.SemaphoreType.DMA((5,))],
        compiler_params=pltpu.CompilerParams(vmem_limit_bytes=3 * MIB),
        cost_estimate=pl.CostEstimate(flops=0, bytes_accessed=3 * MIB, transcendentals=0),
    )(blocks, inverse)


def choose_kernel(chosen, plane_ref, here_ref, else_ref, out_ref, sems):
    for k in range(3):
        part = pl.ds(3 * k, 3)

        @pl.when(plane_ref[0] == chosen)
        def _():
            pltpu.make_async_copy(here_ref.at[part], out_ref.at[part], sems.at[k]).start()

        @pl.when(plane_ref[0] != chosen)
        def _():
            pltpu.make_async_copy(else_ref.at[part], out_ref.at[part], sems.at[k]).start()

    for k in range(3):
        part = pl.ds(3 * k, 3)
        pltpu.make_async_copy(else_ref.at[part], out_ref.at[part], sems.at[k]).wait()


def choose(plane, chosen, here, otherwise):
    return pl.pallas_call(
        functools.partial(choose_kernel, chosen),
        in_specs=[SMEM, ANY, ANY],
        out_specs=VM,
        out_shape=jax.ShapeDtypeStruct((PACKED, WIDTH, WIDTH), BF),
        scratch_shapes=[pltpu.SemaphoreType.DMA((3,))],
        compiler_params=pltpu.CompilerParams(vmem_limit_bytes=3 * MIB),
        cost_estimate=pl.CostEstimate(flops=0, bytes_accessed=3 * MIB, transcendentals=0),
    )(plane, here, otherwise)


WHERE = {
    0: ([0, 2, 4, 5], [1, 4, 5, 3]),
    1: ([5, 0, 2, 4], [3, 1, 6, 7]),
    2: ([4, 5, 0, 2], [7, 3, 1, 6]),
    3: ([2, 6, 7, 0], [6, 7, 3, 1]),
}


def used(level):
    return sorted(set(WHERE[level][0] + WHERE[level][1]))


def factor_copies(level, plane, refs, buf, sems):
    names = used(level)

    def copy(n, z):
        src = refs[len(names) * (n // 2) + names.index(WHERE[level][n % 2][z])]
        return pltpu.make_async_copy(src.at[FAN] if level == 3 else src, buf.at[n], sems.at[n])

    for z in range(4):

        @pl.when(plane == z)
        def _():
            for n in range(4):
                copy(n, z).start()

    return [copy(n, 0) for n in range(4)]


def told_by(plane, level):
    return jnp.bitwise_and(plane - level + 4, 3)


def add_terms(n, at_ref, came, solved, buf, acc_ref):
    terms = dot_t(solved, buf[n, :FAN].reshape(FAN * WIDTH, WIDTH))
    for p in range(FAN):
        acc_ref[at_ref[came, n, p]] += terms[:, p * WIDTH : (p + 1) * WIDTH]


def row_copies(came, refs, rows, sems):
    copies = []
    for r in range(2):
        src = refs[r].at[came, pl.ds((KEEP, SEND)[r], 2 * COLS)]
        copies.append(pltpu.make_async_copy(src, rows.at[pl.ds(2 * COLS * r, 2 * COLS)], sems.at[r]))
        copies[r].start()
    return copies


def rows_of(buf, n, size):
    return buf[n * size : (n + 1) * size]


def inflow_kernel(got_ref, out_ref):
    out_ref[...] = jnp.sum(got_ref[...].astype(F32), axis=0)


def inflow_of(got):
    return pl.pallas_call(
        inflow_kernel,
        in_specs=[VM],
        out_specs=VM,
        out_shape=NODE_F32,
        compiler_params=pltpu.CompilerParams(vmem_limit_bytes=4 * MIB),
        cost_estimate=pl.CostEstimate(flops=MIB, bytes_accessed=MIB, transcendentals=0),
    )(got)


def forward_kernel(level, plane_ref, at_ref, *rest):
    gots, rest = (rest[:1], rest[1:]) if level else ((), rest)
    told, refs, (f_ref, fb_ref, share_ref, rows, rsems, buf, sems, acc_ref) = rest[:2], rest[2:-8], rest[-8:]
    came = told_by(plane_ref[0], level)
    copies_r = row_copies(came, told, rows, rsems)
    copies = factor_copies(level, plane_ref[0], refs, buf, sems)
    acc_ref[...] = jnp.zeros_like(acc_ref)
    for copy in copies_r:
        copy.wait()
    solved = []
    for n in range(4):
        resid = rows_of(rows, n, COLS)
        if level:
            inflow = gots[0][n] if level == 1 else jnp.sum(gots[0][:, n].astype(F32), axis=0)
            resid = (resid.astype(F32) - inflow).astype(BF)
        copies[n].wait()
        f = dot_t(resid, buf[n, FAN])
        f_ref[n] = f
        solved.append(f.astype(BF))
        fb_ref[n] = solved[n]
    for n in range(4):
        add_terms(n, at_ref, came, solved[n], buf, acc_ref)
    share_ref[...] = acc_ref[...].astype(BF)


SMALL = [
    pltpu.VMEM((4 * COLS, WIDTH), BF),
    pltpu.SemaphoreType.DMA((2,)),
]
LARGE = [
    pltpu.VMEM((4, PACKED, WIDTH, WIDTH), BF),
    pltpu.SemaphoreType.DMA((4,)),
]
NODE_F32 = jax.ShapeDtypeStruct((4, COLS, WIDTH), F32)
NODE_BF = jax.ShapeDtypeStruct((4, COLS, WIDTH), BF)
COPIES = jax.ShapeDtypeStruct((CHIPS, 4, COLS, WIDTH), BF)


def pick(level, factors):
    return [factors[r][k] for r in range(2) for k in used(level)]


def forward_level(level, plane, at, gots, told, factors):
    blocks = pick(level, factors)
    return pl.pallas_call(
        functools.partial(forward_kernel, level),
        in_specs=[SMEM, SMEM] + [VM] * len(gots) + any_specs(2) + [ANY] * len(blocks),
        out_specs=(VM, VM, VM),
        scratch_shapes=SMALL + LARGE + [pltpu.VMEM((NODES, COLS, WIDTH), F32)],
        out_shape=(NODE_F32, NODE_BF, jax.ShapeDtypeStruct((NODES, COLS, WIDTH), BF)),
        compiler_params=pltpu.CompilerParams(vmem_limit_bytes=LIMIT),
        cost_estimate=pl.CostEstimate(flops=2 * 36 * COLS * WIDTH**2, bytes_accessed=6 * MIB, transcendentals=0),
    )(plane, at, *gots, *told, *blocks)


def top_kernel(plane_ref, got_ref, own_told, other_told, *rest):
    refs, (fb_ref, sol_ref, copies_ref, rows, rsems, invs, sems) = rest[:-7], rest[-7:]
    copies_r = row_copies(told_by(plane_ref[0], 3), (own_told, other_told), rows, rsems)
    copies = factor_copies(3, plane_ref[0], refs, invs, sems)
    for copy in copies_r:
        copy.wait()
    for n in range(4):
        inflow = jnp.sum(got_ref[:, n].astype(F32), axis=0)
        resid = (rows_of(rows, n, COLS).astype(F32) - inflow).astype(BF)
        copies[n].wait()
        inv = invs[n]
        fb = dot_t(resid, inv).astype(BF)
        fb_ref[n] = fb
        sol = dot_n(fb, inv).astype(BF)
        sol_ref[n] = sol
        for k in range(CHIPS):
            copies_ref[k, n] = sol


def top_level(plane, got, told, factors):
    blocks = pick(3, factors)
    return pl.pallas_call(
        top_kernel,
        in_specs=[SMEM, VM] + any_specs(2 + len(blocks)),
        out_specs=(VM, VM, VM),
        scratch_shapes=SMALL + [pltpu.VMEM((4, WIDTH, WIDTH), BF), pltpu.SemaphoreType.DMA((4,))],
        out_shape=(NODE_BF, NODE_BF, COPIES),
        compiler_params=pltpu.CompilerParams(vmem_limit_bytes=8 * MIB),
        cost_estimate=pl.CostEstimate(flops=2 * 8 * COLS * WIDTH**2, bytes_accessed=3 * MIB, transcendentals=0),
    )(plane, got, *told, *blocks)


def backward_kernel(level, plane_ref, at_ref, above_ref, f_ref, *rest):
    count = 2 * len(used(level))
    refs, outs, (buf, sems) = rest[:count], rest[count:-2], rest[-2:]
    copies = factor_copies(level, plane_ref[0], refs, buf, sems)
    came = told_by(plane_ref[0], level)
    uppers = []
    for n in range(4):
        picked = jnp.concatenate([above_ref[at_ref[came, n, p]] for p in range(FAN)], axis=1)
        copies[n].wait()
        back = dot_n(picked, buf[n, :FAN].reshape(FAN * WIDTH, WIDTH))
        uppers.append((f_ref[n] - back).astype(BF))
    for n in range(4):
        sol = dot_n(uppers[n], buf[n, FAN]).astype(BF)
        outs[0][n] = sol
        if level:
            for k in range(CHIPS):
                outs[1][k, n] = sol


def backward_level(level, plane, at, above, f, factors):
    blocks = pick(level, factors)
    out_shape = (NODE_BF, COPIES) if level else (NODE_BF,)
    return pl.pallas_call(
        functools.partial(backward_kernel, level),
        in_specs=[SMEM, SMEM, VM, VM] + any_specs(len(blocks)),
        out_specs=(VM,) * len(out_shape),
        scratch_shapes=LARGE,
        out_shape=out_shape,
        compiler_params=pltpu.CompilerParams(vmem_limit_bytes=LIMIT),
        cost_estimate=pl.CostEstimate(flops=2 * 36 * COLS * WIDTH**2, bytes_accessed=6 * MIB, transcendentals=0),
    )(plane, at, above, f, *blocks)


def last_kernel(core_ref, fx_ref, forward_ref, result_ref):
    core = core_ref[0]
    for k, out_ref in enumerate((forward_ref, result_ref)):
        for j in range(2):
            halves = []
            for half in range(2):
                rel = jnp.bitwise_xor(core, half)
                halves += [fx_ref[z, rel, k, j] for z in range(4)]
            out_ref[j] = jnp.transpose(jnp.concatenate(halves, axis=0).astype(F32))


def last_step(core, fx):
    return pl.pallas_call(
        last_kernel,
        out_shape=(jax.ShapeDtypeStruct((2, WIDTH, WIDTH), F32),) * 2,
        in_specs=[SMEM, VM],
        out_specs=(VM, VM),
        compiler_params=pltpu.CompilerParams(vmem_limit_bytes=8 * MIB),
        cost_estimate=pl.CostEstimate(flops=0, bytes_accessed=2 * 2**20, transcendentals=0),
    )(core, fx)


def swap(value):
    return lax.ppermute(value, "c", [(0, 1), (1, 0)])


def exchange(value):
    return lax.all_to_all(value.reshape(CHIPS, 4, COLS, WIDTH), ("x", "y"), 0, 0, tiled=True)


def on_device(rhs, inverses, blocks, pattern):
    core = lax.axis_index("c").astype(jnp.int32)
    plane = lax.axis_index("z").astype(jnp.int32)
    core1, plane1 = core.reshape(1), plane.reshape(1)
    factor = blocks.reshape(2, FAN, WIDTH, WIDTH)
    inverse = inverses.reshape(2, WIDTH, WIDTH)

    with jax.named_scope("tell_planes"):
        pat = jnp.pad(pattern.reshape(2, FAN).astype(BF), ((0, ROWS - PAT - 2), (0, WIDTH - FAN)))
        message = pack(core1, plane1, rhs.reshape(2, WIDTH, WIDTH), pat)
        told = [message[0]]
        for k in range(1, 4):
            told.append(lax.ppermute(message[k], "z", [(z, (z + k) % 4) for z in range(4)]))

    with jax.named_scope("factor_step_1"):
        own_a, own_b = join(0, factor, inverse), join(1, factor, inverse)
        own_a, own_b, told = lax.optimization_barrier((own_a, own_b, told))
        up_1 = lax.ppermute(own_a, "z", UP)
        down_1 = lax.ppermute(own_b, "z", DOWN)
        near_a, near_b = swap(own_a), swap(own_b)

    with jax.named_scope("tell_planes"):
        told = jnp.stack(told)
        told = (told, swap(told))
        targets = jnp.concatenate([t[:, PAT : PAT + 2, :FAN] for t in told], axis=1).astype(jnp.int32)
        targets = jnp.clip(targets, 0, NODES - 1)
        places = (targets % 32) // 2 * 4 + jnp.bitwise_xor(targets % 2, core) * 2 + targets // 32

    with jax.named_scope("factor_step_2"):
        up_2 = lax.ppermute(choose(plane1, 0, own_b, up_1), "z", UP)
        down_2 = lax.ppermute(choose(plane1, 3, down_1, own_a), "z", DOWN)
        up_3 = choose(plane1, 0, up_1, own_b)
        down_3 = choose(plane1, 3, own_a, down_1)
        near = (near_a, near_b, swap(up_1), swap(down_1))
        up_2, down_2, up_3, down_3, told, places, near = lax.optimization_barrier(
            (up_2, down_2, up_3, down_3, told, places, near)
        )
        near += (swap(up_2), swap(down_2))
    with jax.named_scope("factor_step_3"):
        up_3 = lax.ppermute(up_3, "z", UP)
        down_3 = lax.ppermute(down_3, "z", DOWN)

    factors = ([own_a, own_b, up_1, down_1, up_2, down_2], list(near))
    forward = [None] * 3
    solved = [None] * 4
    gots = ()
    for level in range(3):
        with jax.named_scope(f"forward_{level}"):
            forward[level], solved[level], share = forward_level(level, plane1, places, gots, told, factors)
            got = exchange(share)
        if level == 0:
            with jax.named_scope("factor_step_3"):
                up_3, down_3, got = lax.optimization_barrier((up_3, down_3, inflow_of(got)))
                factors[0].extend([up_3, down_3])
                factors[1].extend([swap(up_3), swap(down_3)])
        gots = (got,)
    result = [None] * 4
    with jax.named_scope("top"):
        solved[3], result[3], copies = top_level(plane1, got, told, factors)

    for level in (2, 1, 0):
        with jax.named_scope(f"backward_{level}"):
            above = exchange(copies).reshape(NODES, COLS, WIDTH)
            out = backward_level(level, plane1, places, above, forward[level], factors)
            result[level] = out[0]
            if level > 0:
                copies = out[1]

    with jax.named_scope("to_planes"):
        fx = jnp.stack([jnp.stack(solved), jnp.stack(result)], axis=1).reshape(4, 2, 2, 2, COLS, WIDTH)
        fx = jnp.stack([fx[:, :, 0], swap(fx[:, :, 1])], axis=1)
        fx = lax.all_to_all(fx, "z", 0, 0, tiled=True)
        forward_out, result_out = last_step(core1, fx)
    shape = (1, 2, 1, WIDTH, WIDTH)
    return forward_out.reshape(shape), result_out.reshape(shape)


def solution(mesh):
    wide = Mesh(mesh.devices.reshape(4, 4, 2, 4), ("x", "y", "c", "z"))
    blk = ("x", "y", "c")
    return jax.shard_map(
        on_device,
        mesh=wide,
        in_specs=(
            P("z", None, blk, None, None),
            P("z", None, blk, None, None),
            P("z", None, blk, None, None, None),
            P("z", None, blk, None),
        ),
        out_specs=(P("z", None, blk, None, None), P("z", None, blk, None, None)),
        check_vma=False,
    )
```

```python
import functools

import jax
import jax.numpy as jnp
from jax import lax
from jax.experimental import pallas as pl
from jax.experimental.pallas import tpu as pltpu
from jax.sharding import Mesh, PartitionSpec as P


BF = jnp.bfloat16
F32 = jnp.float32
MIB = 1024 * 1024
LIMIT = 14 * MIB
NODES = 64
CHIPS = 16
WIDTH = 256
FAN = 8
HALF = 128
COLS = 32
UP = [(z, (z + 1) % 4) for z in range(4)]
DOWN = [(z, (z + 3) % 4) for z in range(4)]


SMEM = pl.BlockSpec(memory_space=pltpu.SMEM)
VM = pl.BlockSpec(memory_space=pltpu.VMEM)


def dot_t(a, b):
    return lax.dot_general(a, b, (((1,), (1,)), ((), ())), preferred_element_type=F32)


def dot_n(a, b):
    return lax.dot_general(a, b, (((1,), (0,)), ((), ())), preferred_element_type=F32)


KEEP, SEND, PAT, ROWS = 0, 64, 128, 144


def pack_kernel(core_ref, plane_ref, pat_ref, rhs_ref, out_ref):
    core, plane = core_ref[0], plane_ref[0]
    row = lax.broadcasted_iota(jnp.int32, (ROWS - PAT, WIDTH), 0)
    col = lax.broadcasted_iota(jnp.int32, (ROWS - PAT, WIDTH), 1)
    pat = jnp.zeros((ROWS - PAT, WIDTH), F32)
    for j in range(2):
        for p in range(FAN):
            pat = jnp.where((row == j) & (col == p), pat_ref[j, p].astype(F32), pat)
    for k in range(4):
        out_ref[k, PAT:ROWS] = pat.astype(BF)
    for j in range(2):
        rt = jnp.transpose(rhs_ref[j]).astype(BF)
        for half in range(2):
            at = pl.multiple_of(jnp.where(core == half, KEEP, SEND) + j * COLS, COLS)
            for z in range(4):
                first = half * HALF + z * COLS
                out_ref[jnp.bitwise_and(z - plane + 4, 3), pl.ds(at, COLS)] = rt[first : first + COLS]


def pack(core, plane, pat, rhs):
    return pl.pallas_call(
        pack_kernel,
        out_shape=jax.ShapeDtypeStruct((4, ROWS, WIDTH), BF),
        in_specs=[SMEM, SMEM, SMEM, VM],
        out_specs=VM,
        compiler_params=pltpu.CompilerParams(vmem_limit_bytes=8 * MIB),
        cost_estimate=pl.CostEstimate(flops=0, bytes_accessed=2 * MIB, transcendentals=0),
    )(core, plane, pat, rhs)


ANY = pl.BlockSpec(memory_space=pl.ANY)


def any_specs(count):
    return [ANY] * count


PACKED = FAN + 1


def join_kernel(j, blocks_ref, inv_ref, out_ref, sems):
    copies = [pltpu.make_async_copy(inv_ref.at[j], out_ref.at[FAN], sems.at[0])]
    for k in range(4):
        part = pl.ds(2 * k, 2)
        copies.append(pltpu.make_async_copy(blocks_ref.at[j, part], out_ref.at[part], sems.at[1 + k]))
    for copy in copies:
        copy.start()
    for copy in copies:
        copy.wait()


def join(j, blocks, inverse):
    return pl.pallas_call(
        functools.partial(join_kernel, j),
        in_specs=[ANY, ANY],
        out_specs=VM,
        out_shape=jax.ShapeDtypeStruct((PACKED, WIDTH, WIDTH), BF),
        scratch_shapes=[pltpu.SemaphoreType.DMA((5,))],
        compiler_params=pltpu.CompilerParams(vmem_limit_bytes=3 * MIB),
        cost_estimate=pl.CostEstimate(flops=0, bytes_accessed=3 * MIB, transcendentals=0),
    )(blocks, inverse)


def choose_kernel(chosen, plane_ref, here_ref, else_ref, out_ref, sems):
    for k in range(3):
        part = pl.ds(3 * k, 3)

        @pl.when(plane_ref[0] == chosen)
        def _():
            pltpu.make_async_copy(here_ref.at[part], out_ref.at[part], sems.at[k]).start()

        @pl.when(plane_ref[0] != chosen)
        def _():
            pltpu.make_async_copy(else_ref.at[part], out_ref.at[part], sems.at[k]).start()

    for k in range(3):
        part = pl.ds(3 * k, 3)
        pltpu.make_async_copy(else_ref.at[part], out_ref.at[part], sems.at[k]).wait()


def choose(plane, chosen, here, otherwise):
    return pl.pallas_call(
        functools.partial(choose_kernel, chosen),
        in_specs=[SMEM, ANY, ANY],
        out_specs=VM,
        out_shape=jax.ShapeDtypeStruct((PACKED, WIDTH, WIDTH), BF),
        scratch_shapes=[pltpu.SemaphoreType.DMA((3,))],
        compiler_params=pltpu.CompilerParams(vmem_limit_bytes=3 * MIB),
        cost_estimate=pl.CostEstimate(flops=0, bytes_accessed=3 * MIB, transcendentals=0),
    )(plane, here, otherwise)


WHERE = {
    0: ([0, 2, 4, 5], [1, 4, 5, 3]),
    1: ([5, 0, 2, 4], [3, 1, 6, 7]),
    2: ([4, 5, 0, 2], [7, 3, 1, 6]),
    3: ([2, 6, 7, 0], [6, 7, 3, 1]),
}


def used(level):
    return sorted(set(WHERE[level][0] + WHERE[level][1]))


def factor_copies(level, plane, refs, buf, sems, nodes=(0, 1, 2, 3)):
    names = used(level)

    def copy(n, z):
        src = refs[len(names) * (n // 2) + names.index(WHERE[level][n % 2][z])]
        return pltpu.make_async_copy(src.at[FAN] if level == 3 else src, buf.at[n], sems.at[n])

    for z in range(4):

        @pl.when(plane == z)
        def _():
            for n in nodes:
                copy(n, z).start()

    return {n: copy(n, 0) for n in nodes}


def told_by(plane, level):
    return jnp.bitwise_and(plane - level + 4, 3)


def add_terms(n, at_ref, came, solved, block, acc_ref):
    terms = dot_t(solved, block[:FAN].reshape(FAN * WIDTH, WIDTH))
    for p in range(FAN):
        acc_ref[at_ref[came, n, p]] += terms[:, p * WIDTH : (p + 1) * WIDTH]


def row_copies(came, refs, rows, sems, cores=(0, 1)):
    copies = []
    for r in cores:
        src = refs[r].at[came, pl.ds((KEEP, SEND)[r], 2 * COLS)]
        copies.append(pltpu.make_async_copy(src, rows.at[pl.ds(2 * COLS * r, 2 * COLS)], sems.at[r]))
        copies[-1].start()
    return copies


def rows_of(buf, n, size):
    return buf[n * size : (n + 1) * size]


def inflow_kernel(got_ref, out_ref):
    out_ref[...] = jnp.sum(got_ref[...].astype(F32), axis=0)


def inflow_of(got):
    return pl.pallas_call(
        inflow_kernel,
        in_specs=[VM],
        out_specs=VM,
        out_shape=NODE_F32,
        compiler_params=pltpu.CompilerParams(vmem_limit_bytes=4 * MIB),
        cost_estimate=pl.CostEstimate(flops=MIB, bytes_accessed=MIB, transcendentals=0),
    )(got)


def forward_kernel(level, part, core_ref, plane_ref, at_ref, *rest):
    gots, rest = (rest[:1], rest[1:]) if level else ((), rest)
    before, rest = (rest[:3], rest[3:]) if part == 1 else ((), rest)
    told, refs, (f_ref, fb_ref, out_ref, rows, rsems, buf, sems, acc_ref) = rest[:2], rest[2:-8], rest[-8:]
    came = told_by(plane_ref[0], level)
    copies_r = row_copies(came, told, rows, rsems)

    def run(nodes):
        copies = factor_copies(level, plane_ref[0], refs, buf, sems, nodes)
        solved = {}
        for n in nodes:
            resid = rows_of(rows, n, COLS)
            if level:
                inflow = gots[0][n] if level == 1 else jnp.sum(gots[0][:, n].astype(F32), axis=0)
                resid = (resid.astype(F32) - inflow).astype(BF)
            copies[n].wait()
            f = dot_t(resid, buf[n, FAN])
            f_ref[n] = f
            solved[n] = f.astype(BF)
            fb_ref[n] = solved[n]
        for n in nodes:
            add_terms(n, at_ref, came, solved[n], buf.at[n], acc_ref)

    if part == 1:
        f_ref[...], fb_ref[...], acc_ref[...] = before[0][...], before[1][...], before[2][...]
    else:
        acc_ref[...] = jnp.zeros_like(acc_ref)
    for copy in copies_r:
        copy.wait()
    if part is None:
        run((0, 1, 2, 3))
    elif part == 0:
        f_ref[...], fb_ref[...] = jnp.zeros_like(f_ref), jnp.zeros_like(fb_ref)
        pl.when(core_ref[0] == 1)(lambda: run((0, 1, 2)))
    else:
        pl.when(core_ref[0] == 1)(lambda: run((3,)))
        pl.when(core_ref[0] == 0)(lambda: run((0, 1, 2, 3)))
    out_ref[...] = acc_ref[...].astype(out_ref.dtype)


SMALL = [
    pltpu.VMEM((4 * COLS, WIDTH), BF),
    pltpu.SemaphoreType.DMA((2,)),
]
LARGE = [
    pltpu.VMEM((4, PACKED, WIDTH, WIDTH), BF),
    pltpu.SemaphoreType.DMA((4,)),
]
NODE_F32 = jax.ShapeDtypeStruct((4, COLS, WIDTH), F32)
NODE_BF = jax.ShapeDtypeStruct((4, COLS, WIDTH), BF)
COPIES = jax.ShapeDtypeStruct((CHIPS, 4, COLS, WIDTH), BF)


def pick(level, factors):
    return [factors[r][k] for r in range(2) for k in used(level)]


def forward_part(level, part, here, at, gots, before, told, blocks):
    last = jax.ShapeDtypeStruct((NODES, COLS, WIDTH), F32 if part == 0 else BF)
    return pl.pallas_call(
        functools.partial(forward_kernel, level, part),
        in_specs=[SMEM] * 3 + [VM] * (len(gots) + len(before)) + any_specs(2 + len(blocks)),
        out_specs=(VM, VM, VM),
        scratch_shapes=SMALL + LARGE + [pltpu.VMEM((NODES, COLS, WIDTH), F32)],
        out_shape=(NODE_F32, NODE_BF, last),
        compiler_params=pltpu.CompilerParams(vmem_limit_bytes=LIMIT),
        cost_estimate=pl.CostEstimate(flops=2 * 36 * COLS * WIDTH**2, bytes_accessed=6 * MIB, transcendentals=0),
    )(*here, at, *gots, *before, *told, *blocks)


def forward_level(level, here, at, gots, told, factors):
    return forward_part(level, None, here, at, gots, (), told, pick(level, factors))


def forward_halves(level, here, at, gots, told, factors):
    early = [factors[0][k] for k in used(level)] + [factors[1][k] for k in used(level) if k < 6]
    before = forward_part(level, 0, here, at, gots, (), told, early)
    return forward_part(level, 1, here, at, gots, before, told, pick(level, factors))


def top_kernel(plane_ref, got_ref, own_told, other_told, *rest):
    refs, (fb_ref, sol_ref, copies_ref, rows, rsems, invs, sems) = rest[:-7], rest[-7:]
    copies_r = row_copies(told_by(plane_ref[0], 3), (own_told, other_told), rows, rsems)
    copies = factor_copies(3, plane_ref[0], refs, invs, sems)
    for copy in copies_r:
        copy.wait()
    for n in range(4):
        inflow = jnp.sum(got_ref[:, n].astype(F32), axis=0)
        resid = (rows_of(rows, n, COLS).astype(F32) - inflow).astype(BF)
        copies[n].wait()
        inv = invs[n]
        fb = dot_t(resid, inv).astype(BF)
        fb_ref[n] = fb
        sol = dot_n(fb, inv).astype(BF)
        sol_ref[n] = sol
        for k in range(CHIPS):
            copies_ref[k, n] = sol


def top_level(plane, got, told, factors):
    blocks = pick(3, factors)
    return pl.pallas_call(
        top_kernel,
        in_specs=[SMEM, VM] + any_specs(2 + len(blocks)),
        out_specs=(VM, VM, VM),
        scratch_shapes=SMALL + [pltpu.VMEM((4, WIDTH, WIDTH), BF), pltpu.SemaphoreType.DMA((4,))],
        out_shape=(NODE_BF, NODE_BF, COPIES),
        compiler_params=pltpu.CompilerParams(vmem_limit_bytes=8 * MIB),
        cost_estimate=pl.CostEstimate(flops=2 * 8 * COLS * WIDTH**2, bytes_accessed=3 * MIB, transcendentals=0),
    )(plane, got, *told, *blocks)


def backward_kernel(level, plane_ref, at_ref, above_ref, f_ref, *rest):
    count = 2 * len(used(level))
    refs, outs, (buf, sems) = rest[:count], rest[count:-2], rest[-2:]
    copies = factor_copies(level, plane_ref[0], refs, buf, sems)
    came = told_by(plane_ref[0], level)
    uppers = []
    for n in range(4):
        picked = jnp.concatenate([above_ref[at_ref[came, n, p]] for p in range(FAN)], axis=1)
        copies[n].wait()
        back = dot_n(picked, buf[n, :FAN].reshape(FAN * WIDTH, WIDTH))
        uppers.append((f_ref[n] - back).astype(BF))
    for n in range(4):
        sol = dot_n(uppers[n], buf[n, FAN]).astype(BF)
        outs[0][n] = sol
        if level:
            for k in range(CHIPS):
                outs[1][k, n] = sol


def backward_level(level, plane, at, above, f, factors):
    blocks = pick(level, factors)
    out_shape = (NODE_BF, COPIES) if level else (NODE_BF,)
    return pl.pallas_call(
        functools.partial(backward_kernel, level),
        in_specs=[SMEM, SMEM, VM, VM] + any_specs(len(blocks)),
        out_specs=(VM,) * len(out_shape),
        scratch_shapes=LARGE,
        out_shape=out_shape,
        compiler_params=pltpu.CompilerParams(vmem_limit_bytes=LIMIT),
        cost_estimate=pl.CostEstimate(flops=2 * 36 * COLS * WIDTH**2, bytes_accessed=6 * MIB, transcendentals=0),
    )(plane, at, above, f, *blocks)


def last_kernel(core_ref, fx_ref, forward_ref, result_ref):
    core = core_ref[0]
    for k, out_ref in enumerate((forward_ref, result_ref)):
        for j in range(2):
            halves = []
            for half in range(2):
                rel = jnp.bitwise_xor(core, half)
                halves += [fx_ref[z, rel, k, j] for z in range(4)]
            out_ref[j] = jnp.transpose(jnp.concatenate(halves, axis=0).astype(F32))


def last_step(core, fx):
    return pl.pallas_call(
        last_kernel,
        out_shape=(jax.ShapeDtypeStruct((2, WIDTH, WIDTH), F32),) * 2,
        in_specs=[SMEM, VM],
        out_specs=(VM, VM),
        compiler_params=pltpu.CompilerParams(vmem_limit_bytes=8 * MIB),
        cost_estimate=pl.CostEstimate(flops=0, bytes_accessed=2 * 2**20, transcendentals=0),
    )(core, fx)


def swap(value):
    return lax.ppermute(value, "c", [(0, 1), (1, 0)])


def exchange(value):
    return lax.all_to_all(value.reshape(CHIPS, 4, COLS, WIDTH), ("x", "y"), 0, 0, tiled=True)


def on_device(rhs, inverses, blocks, pattern):
    core = lax.axis_index("c").astype(jnp.int32)
    plane = lax.axis_index("z").astype(jnp.int32)
    core1, plane1 = core.reshape(1), plane.reshape(1)
    factor = blocks.reshape(2, FAN, WIDTH, WIDTH)
    inverse = inverses.reshape(2, WIDTH, WIDTH)

    with jax.named_scope("tell_planes"):
        message = pack(core1, plane1, pattern.reshape(2, FAN), rhs.reshape(2, WIDTH, WIDTH))
        told = [message[0]]
        for k in range(1, 4):
            told.append(lax.ppermute(message[k], "z", [(z, (z + k) % 4) for z in range(4)]))

    with jax.named_scope("factor_step_1"):
        own_a, own_b = join(0, factor, inverse), join(1, factor, inverse)
        own_a, own_b, told = lax.optimization_barrier((own_a, own_b, told))
        up_1 = lax.ppermute(own_a, "z", UP)
        down_1 = lax.ppermute(own_b, "z", DOWN)
        near_a, near_b = swap(own_a), swap(own_b)

    with jax.named_scope("tell_planes"):
        told = jnp.stack(told)
        told = (told, swap(told))
        targets = jnp.concatenate([t[:, PAT : PAT + 2, :FAN] for t in told], axis=1).astype(jnp.int32)
        targets = jnp.clip(targets, 0, NODES - 1)
        places = (targets % 32) // 2 * 4 + jnp.bitwise_xor(targets % 2, core) * 2 + targets // 32

    with jax.named_scope("factor_step_2"):
        up_2 = lax.ppermute(choose(plane1, 0, own_b, up_1), "z", UP)
        down_2 = lax.ppermute(choose(plane1, 3, down_1, own_a), "z", DOWN)
        up_3 = choose(plane1, 0, up_1, own_b)
        down_3 = choose(plane1, 3, own_a, down_1)
        near = (near_a, near_b, swap(up_1), swap(down_1))
        up_2, down_2, up_3, down_3, told, places, near = lax.optimization_barrier(
            (up_2, down_2, up_3, down_3, told, places, near)
        )
        near += (swap(up_2), swap(down_2))
    with jax.named_scope("factor_step_3"):
        up_3 = lax.ppermute(up_3, "z", UP)
        down_3 = lax.ppermute(down_3, "z", DOWN)

    factors = ([own_a, own_b, up_1, down_1, up_2, down_2], list(near))
    forward = [None] * 3
    solved = [None] * 4
    gots = ()
    for level in range(3):
        with jax.named_scope(f"forward_{level}"):
            solve = forward_halves if level == 1 else forward_level
            forward[level], solved[level], share = solve(level, (core1, plane1), places, gots, told, factors)
            got = exchange(share)
        if level == 0:
            with jax.named_scope("factor_step_3"):
                up_3, down_3, got = lax.optimization_barrier((up_3, down_3, inflow_of(got)))
                factors[0].extend([up_3, down_3])
                factors[1].extend([swap(up_3), swap(down_3)])
        gots = (got,)
    result = [None] * 4
    with jax.named_scope("top"):
        solved[3], result[3], copies = top_level(plane1, got, told, factors)

    for level in (2, 1, 0):
        with jax.named_scope(f"backward_{level}"):
            above = exchange(copies).reshape(NODES, COLS, WIDTH)
            out = backward_level(level, plane1, places, above, forward[level], factors)
            result[level] = out[0]
            if level > 0:
                copies = out[1]

    with jax.named_scope("to_planes"):
        fx = jnp.stack([jnp.stack(solved), jnp.stack(result)], axis=1).reshape(4, 2, 2, 2, COLS, WIDTH)
        fx = jnp.stack([fx[:, :, 0], swap(fx[:, :, 1])], axis=1)
        fx = lax.all_to_all(fx, "z", 0, 0, tiled=True)
        forward_out, result_out = last_step(core1, fx)
    shape = (1, 2, 1, WIDTH, WIDTH)
    return forward_out.reshape(shape), result_out.reshape(shape)


def solution(mesh):
    wide = Mesh(mesh.devices.reshape(4, 4, 2, 4), ("x", "y", "c", "z"))
    blk = ("x", "y", "c")
    return jax.shard_map(
        on_device,
        mesh=wide,
        in_specs=(
            P("z", None, blk, None, None),
            P("z", None, blk, None, None),
            P("z", None, blk, None, None, None),
            P("z", None, blk, None),
        ),
        out_specs=(P("z", None, blk, None, None), P("z", None, blk, None, None)),
        check_vma=False,
    )
```

```python
import functools

import jax
import jax.numpy as jnp
from jax import lax
from jax.experimental import pallas as pl
from jax.experimental.pallas import tpu as pltpu
from jax.sharding import Mesh, PartitionSpec as P


BF = jnp.bfloat16
F32 = jnp.float32
MIB = 1024 * 1024
LIMIT = 14 * MIB
NODES = 64
CHIPS = 16
WIDTH = 256
FAN = 8
HALF = 128
COLS = 32
UP = [(z, (z + 1) % 4) for z in range(4)]
DOWN = [(z, (z + 3) % 4) for z in range(4)]


SMEM = pl.BlockSpec(memory_space=pltpu.SMEM)
VM = pl.BlockSpec(memory_space=pltpu.VMEM)


def dot_t(a, b):
    return lax.dot_general(a, b, (((1,), (1,)), ((), ())), preferred_element_type=F32)


def dot_n(a, b):
    return lax.dot_general(a, b, (((1,), (0,)), ((), ())), preferred_element_type=F32)


KEEP, SEND, PAT, ROWS = 0, 64, 128, 144


def pack_kernel(core_ref, plane_ref, pat_ref, rhs_ref, out_ref):
    core, plane = core_ref[0], plane_ref[0]
    row = lax.broadcasted_iota(jnp.int32, (ROWS - PAT, WIDTH), 0)
    col = lax.broadcasted_iota(jnp.int32, (ROWS - PAT, WIDTH), 1)
    pat = jnp.zeros((ROWS - PAT, WIDTH), F32)
    for j in range(2):
        for p in range(FAN):
            pat = jnp.where((row == j) & (col == p), pat_ref[j, p].astype(F32), pat)
    for k in range(4):
        out_ref[k, PAT:ROWS] = pat.astype(BF)
    for j in range(2):
        rt = jnp.transpose(rhs_ref[j]).astype(BF)
        for half in range(2):
            at = pl.multiple_of(jnp.where(core == half, KEEP, SEND) + j * COLS, COLS)
            for z in range(4):
                first = half * HALF + z * COLS
                out_ref[jnp.bitwise_and(z - plane + 4, 3), pl.ds(at, COLS)] = rt[first : first + COLS]


def pack(core, plane, pat, rhs):
    return pl.pallas_call(
        pack_kernel,
        out_shape=jax.ShapeDtypeStruct((4, ROWS, WIDTH), BF),
        in_specs=[SMEM, SMEM, SMEM, VM],
        out_specs=VM,
        compiler_params=pltpu.CompilerParams(vmem_limit_bytes=8 * MIB),
        cost_estimate=pl.CostEstimate(flops=0, bytes_accessed=2 * MIB, transcendentals=0),
    )(core, plane, pat, rhs)


ANY = pl.BlockSpec(memory_space=pl.ANY)


def any_specs(count):
    return [ANY] * count


PACKED = FAN + 1


def join_kernel(j, blocks_ref, inv_ref, out_ref, sems):
    copies = [pltpu.make_async_copy(inv_ref.at[j], out_ref.at[FAN], sems.at[0])]
    for k in range(4):
        part = pl.ds(2 * k, 2)
        copies.append(pltpu.make_async_copy(blocks_ref.at[j, part], out_ref.at[part], sems.at[1 + k]))
    for copy in copies:
        copy.start()
    for copy in copies:
        copy.wait()


def join(j, blocks, inverse):
    return pl.pallas_call(
        functools.partial(join_kernel, j),
        in_specs=[ANY, ANY],
        out_specs=VM,
        out_shape=jax.ShapeDtypeStruct((PACKED, WIDTH, WIDTH), BF),
        scratch_shapes=[pltpu.SemaphoreType.DMA((5,))],
        compiler_params=pltpu.CompilerParams(vmem_limit_bytes=3 * MIB),
        cost_estimate=pl.CostEstimate(flops=0, bytes_accessed=3 * MIB, transcendentals=0),
    )(blocks, inverse)


def choose_kernel(chosen, plane_ref, here_ref, else_ref, out_ref, sems):
    for k in range(3):
        part = pl.ds(3 * k, 3)

        @pl.when(plane_ref[0] == chosen)
        def _():
            pltpu.make_async_copy(here_ref.at[part], out_ref.at[part], sems.at[k]).start()

        @pl.when(plane_ref[0] != chosen)
        def _():
            pltpu.make_async_copy(else_ref.at[part], out_ref.at[part], sems.at[k]).start()

    for k in range(3):
        part = pl.ds(3 * k, 3)
        pltpu.make_async_copy(else_ref.at[part], out_ref.at[part], sems.at[k]).wait()


def choose(plane, chosen, here, otherwise):
    return pl.pallas_call(
        functools.partial(choose_kernel, chosen),
        in_specs=[SMEM, ANY, ANY],
        out_specs=VM,
        out_shape=jax.ShapeDtypeStruct((PACKED, WIDTH, WIDTH), BF),
        scratch_shapes=[pltpu.SemaphoreType.DMA((3,))],
        compiler_params=pltpu.CompilerParams(vmem_limit_bytes=3 * MIB),
        cost_estimate=pl.CostEstimate(flops=0, bytes_accessed=3 * MIB, transcendentals=0),
    )(plane, here, otherwise)


WHERE = {
    0: ([0, 2, 4, 5], [1, 4, 5, 3]),
    1: ([5, 0, 2, 4], [3, 1, 6, 7]),
    2: ([4, 5, 0, 2], [7, 3, 1, 6]),
    3: ([2, 6, 7, 0], [6, 7, 3, 1]),
}


def used(level):
    return sorted(set(WHERE[level][0] + WHERE[level][1]))


def on_plane(plane, run):
    for z in range(4):
        pl.when(plane == z)(functools.partial(run, z))


def told_by(plane, level):
    return jnp.bitwise_and(plane - level + 4, 3)


def add_terms(n, at_ref, came, solved, block, acc_ref):
    terms = dot_t(solved, block[:FAN].reshape(FAN * WIDTH, WIDTH))
    for p in range(FAN):
        acc_ref[at_ref[came, n, p]] += terms[:, p * WIDTH : (p + 1) * WIDTH]


def rows_of(told, came, n):
    return told[n // 2][came, pl.ds((KEEP, SEND)[n // 2] + n % 2 * COLS, COLS)]


def inflow_kernel(got_ref, out_ref):
    out_ref[...] = jnp.sum(got_ref[...].astype(F32), axis=0)


def inflow_of(got):
    return pl.pallas_call(
        inflow_kernel,
        in_specs=[VM],
        out_specs=VM,
        out_shape=NODE_F32,
        compiler_params=pltpu.CompilerParams(vmem_limit_bytes=4 * MIB),
        cost_estimate=pl.CostEstimate(flops=MIB, bytes_accessed=MIB, transcendentals=0),
    )(got)


def forward_kernel(level, part, core_ref, plane_ref, at_ref, *rest):
    gots, rest = (rest[:1], rest[1:]) if level else ((), rest)
    before, rest = (rest[:4], rest[4:]) if part == 1 else ((), rest)
    outs = {None: 4, 0: 5, 1: 6}[part]
    told, refs, (f_ref, fb_ref, share_ref, *extra) = rest[:2], rest[2:-outs], rest[-outs:]
    acc_ref = extra[1 if part == 0 else 0]
    names = used(level)
    came = told_by(plane_ref[0], level)

    def block(n, z):
        return refs[len(names) * (n // 2) + names.index(WHERE[level][n % 2][z])]

    def add(nodes, z, block=block):
        solved = {}
        for n in nodes:
            resid = rows_of(told, came, n)
            if level:
                inflow = gots[0][n] if level == 1 else jnp.sum(gots[0][:, n].astype(F32), axis=0)
                resid = (resid.astype(F32) - inflow).astype(BF)
            f = dot_t(resid, block(n, z)[FAN])
            f_ref[n] = f
            solved[n] = f.astype(BF)
            fb_ref[n] = solved[n]
        for n in nodes:
            add_terms(n, at_ref, came, solved[n], block(n, z), acc_ref)

    def run(nodes):
        acc_ref[...] = jnp.zeros_like(acc_ref)
        on_plane(plane_ref[0], functools.partial(add, nodes))
        share_ref[...] = acc_ref[...].astype(BF)

    def finish(n):
        f_ref[:n], fb_ref[:n] = before[0][:n], before[1][:n]
        targets = [at_ref[came, n, p] for p in range(FAN)]
        for t in targets:
            acc_ref[t] = before[3][t]
        on_plane(plane_ref[0], functools.partial(add, (n,)))
        for t in targets:
            share_ref[t] = acc_ref[t].astype(BF)

    def staged():
        buf, sems = extra[1:]

        def copy(n, z):
            return pltpu.make_async_copy(block(n, z), buf.at[n], sems.at[n])

        def start(z):
            for n in range(4):
                copy(n, z).start()

        on_plane(plane_ref[0], start)
        acc_ref[...] = jnp.zeros_like(acc_ref)
        for n in range(4):
            copy(n, 0).wait()
        add((0, 1, 2, 3), 0, lambda n, z: buf.at[n])
        share_ref[...] = acc_ref[...].astype(BF)

    if part is None:
        run((0, 1, 2, 3))
        return

    @pl.when(core_ref[0] == 1)
    def _():
        if part == 0:
            run((0, 1, 2))
            extra[0][...] = acc_ref[...]
        else:
            finish(3)

    if part == 1:

        @pl.when(core_ref[0] == 0)
        def _():
            staged()


STAGE = [pltpu.VMEM((4, PACKED, WIDTH, WIDTH), BF), pltpu.SemaphoreType.DMA((4,))]
NODE_F32 = jax.ShapeDtypeStruct((4, COLS, WIDTH), F32)
NODE_BF = jax.ShapeDtypeStruct((4, COLS, WIDTH), BF)
COPIES = jax.ShapeDtypeStruct((CHIPS, 4, COLS, WIDTH), BF)


def pick(level, factors):
    return [factors[r][k] for r in range(2) for k in used(level)]


def forward_part(level, part, here, at, gots, before, told, blocks):
    shares = jax.ShapeDtypeStruct((NODES, COLS, WIDTH), BF)
    out_shape = (NODE_F32, NODE_BF, shares)
    if part == 0:
        out_shape += (jax.ShapeDtypeStruct((NODES, COLS, WIDTH), F32),)
    return pl.pallas_call(
        functools.partial(forward_kernel, level, part),
        in_specs=[SMEM] * 3 + [VM] * (len(gots) + len(before) + 2 + len(blocks)),
        out_specs=(VM,) * len(out_shape),
        scratch_shapes=[pltpu.VMEM((NODES, COLS, WIDTH), F32)] + (STAGE if part == 1 else []),
        out_shape=out_shape,
        input_output_aliases={3 + len(gots) + 2: 2} if part == 1 else {},
        compiler_params=pltpu.CompilerParams(vmem_limit_bytes=LIMIT),
        cost_estimate=pl.CostEstimate(flops=2 * 36 * COLS * WIDTH**2, bytes_accessed=6 * MIB, transcendentals=0),
    )(*here, at, *gots, *before, *told, *blocks)


def forward_level(level, here, at, gots, told, factors):
    return forward_part(level, None, here, at, gots, (), told, pick(level, factors))


def forward_halves(level, here, at, gots, told, factors):
    early = [factors[0][k] for k in used(level)] + [factors[1][k] for k in used(level) if k < 6]
    before = forward_part(level, 0, here, at, gots, (), told, early)
    return forward_part(level, 1, here, at, gots, before, told, pick(level, factors))


def top_kernel(plane_ref, got_ref, own_told, other_told, *rest):
    refs, (fb_ref, sol_ref, copies_ref) = rest[:-3], rest[-3:]
    names = used(3)
    came = told_by(plane_ref[0], 3)
    resids = []
    for n in range(4):
        inflow = jnp.sum(got_ref[:, n].astype(F32), axis=0)
        resids.append((rows_of((own_told, other_told), came, n).astype(F32) - inflow).astype(BF))

    def run(z):
        invs = [refs[len(names) * (n // 2) + names.index(WHERE[3][n % 2][z])].at[FAN] for n in range(4)]
        solved = []
        for n in range(4):
            solved.append(dot_t(resids[n], invs[n][...]).astype(BF))
            fb_ref[n] = solved[n]
        for n in range(4):
            sol = dot_n(solved[n], invs[n][...]).astype(BF)
            sol_ref[n] = sol
            for k in range(CHIPS):
                copies_ref[k, n] = sol

    on_plane(plane_ref[0], run)


def top_level(plane, got, told, factors):
    blocks = pick(3, factors)
    return pl.pallas_call(
        top_kernel,
        in_specs=[SMEM] + [VM] * (3 + len(blocks)),
        out_specs=(VM, VM, VM),
        out_shape=(NODE_BF, NODE_BF, COPIES),
        compiler_params=pltpu.CompilerParams(vmem_limit_bytes=LIMIT),
        cost_estimate=pl.CostEstimate(flops=2 * 8 * COLS * WIDTH**2, bytes_accessed=3 * MIB, transcendentals=0),
    )(plane, got, *told, *blocks)


def backward_kernel(level, plane_ref, at_ref, above_ref, f_ref, *rest):
    names = used(level)
    refs, outs = rest[: 2 * len(names)], rest[2 * len(names) :]
    came = told_by(plane_ref[0], level)

    def run(z):
        blocks = [refs[len(names) * (n // 2) + names.index(WHERE[level][n % 2][z])] for n in range(4)]
        uppers = []
        for n in range(4):
            picked = jnp.concatenate([above_ref[at_ref[came, n, p]] for p in range(FAN)], axis=1)
            back = dot_n(picked, blocks[n][:FAN].reshape(FAN * WIDTH, WIDTH))
            uppers.append((f_ref[n] - back).astype(BF))
        for n in range(4):
            sol = dot_n(uppers[n], blocks[n][FAN]).astype(BF)
            outs[0][n] = sol
            if level:
                for k in range(CHIPS):
                    outs[1][k, n] = sol

    on_plane(plane_ref[0], run)


def backward_level(level, plane, at, above, f, factors):
    blocks = pick(level, factors)
    out_shape = (NODE_BF, COPIES) if level else (NODE_BF,)
    return pl.pallas_call(
        functools.partial(backward_kernel, level),
        in_specs=[SMEM, SMEM] + [VM] * (2 + len(blocks)),
        out_specs=(VM,) * len(out_shape),
        out_shape=out_shape,
        compiler_params=pltpu.CompilerParams(vmem_limit_bytes=LIMIT),
        cost_estimate=pl.CostEstimate(flops=2 * 36 * COLS * WIDTH**2, bytes_accessed=6 * MIB, transcendentals=0),
    )(plane, at, above, f, *blocks)


def last_kernel(core_ref, own_ref, other_ref, forward_ref, result_ref):
    core = core_ref[0]
    for k, out_ref in enumerate((forward_ref, result_ref)):
        for j in range(2):
            own = jnp.concatenate([own_ref[z, k, 0, j] for z in range(4)], axis=0).astype(F32)
            other = jnp.concatenate([other_ref[z, k, 1, j] for z in range(4)], axis=0).astype(F32)
            low, high = jnp.where(core == 0, own, other), jnp.where(core == 0, other, own)
            out_ref[j] = jnp.transpose(jnp.concatenate([low, high], axis=0))


def last_step(core, own, other):
    return pl.pallas_call(
        last_kernel,
        out_shape=(jax.ShapeDtypeStruct((2, WIDTH, WIDTH), F32),) * 2,
        in_specs=[SMEM, VM, VM],
        out_specs=(VM, VM),
        compiler_params=pltpu.CompilerParams(vmem_limit_bytes=8 * MIB),
        cost_estimate=pl.CostEstimate(flops=0, bytes_accessed=2 * MIB, transcendentals=0),
    )(core, own, other)


def swap(value):
    return lax.ppermute(value, "c", [(0, 1), (1, 0)])


def exchange(value):
    return lax.all_to_all(value.reshape(CHIPS, 4, COLS, WIDTH), ("x", "y"), 0, 0, tiled=True)


def on_device(rhs, inverses, blocks, pattern):
    core = lax.axis_index("c").astype(jnp.int32)
    plane = lax.axis_index("z").astype(jnp.int32)
    core1, plane1 = core.reshape(1), plane.reshape(1)
    factor = blocks.reshape(2, FAN, WIDTH, WIDTH)
    inverse = inverses.reshape(2, WIDTH, WIDTH)

    with jax.named_scope("tell_planes"):
        message = pack(core1, plane1, pattern.reshape(2, FAN), rhs.reshape(2, WIDTH, WIDTH))
        told = [message[0]]
        for k in range(1, 4):
            told.append(lax.ppermute(message[k], "z", [(z, (z + k) % 4) for z in range(4)]))

    with jax.named_scope("factor_step_1"):
        own_a, own_b = join(0, factor, inverse), join(1, factor, inverse)
        own_a, own_b, told = lax.optimization_barrier((own_a, own_b, told))
        up_1 = lax.ppermute(own_a, "z", UP)
        down_1 = lax.ppermute(own_b, "z", DOWN)
        near_a, near_b = swap(own_a), swap(own_b)

    with jax.named_scope("tell_planes"):
        told = jnp.stack(told)
        told = (told, swap(told))
        targets = jnp.concatenate([t[:, PAT : PAT + 2, :FAN] for t in told], axis=1).astype(jnp.int32)
        targets = jnp.clip(targets, 0, NODES - 1)
        places = (targets % 32) // 2 * 4 + jnp.bitwise_xor(targets % 2, core) * 2 + targets // 32

    with jax.named_scope("factor_step_2"):
        up_2 = lax.ppermute(choose(plane1, 0, own_b, up_1), "z", UP)
        down_2 = lax.ppermute(choose(plane1, 3, down_1, own_a), "z", DOWN)
        up_3 = choose(plane1, 0, up_1, own_b)
        down_3 = choose(plane1, 3, own_a, down_1)
        near = (near_a, near_b, swap(up_1), swap(down_1))
        up_2, down_2, up_3, down_3, told, places, near = lax.optimization_barrier(
            (up_2, down_2, up_3, down_3, told, places, near)
        )
        near += (swap(up_2), swap(down_2))
    with jax.named_scope("factor_step_3"):
        up_3 = lax.ppermute(up_3, "z", UP)
        down_3 = lax.ppermute(down_3, "z", DOWN)

    factors = ([own_a, own_b, up_1, down_1, up_2, down_2], list(near))
    forward = [None] * 3
    solved = [None] * 4
    gots = ()
    for level in range(3):
        with jax.named_scope(f"forward_{level}"):
            solve = forward_halves if level == 1 else forward_level
            forward[level], solved[level], share = solve(level, (core1, plane1), places, gots, told, factors)
            got = exchange(share)
        if level == 0:
            with jax.named_scope("factor_step_3"):
                up_3, down_3, got = lax.optimization_barrier((up_3, down_3, inflow_of(got)))
                factors[0].extend([up_3, down_3])
                factors[1].extend([swap(up_3), swap(down_3)])
        gots = (got,)
    result = [None] * 4
    with jax.named_scope("top"):
        solved[3], result[3], copies = top_level(plane1, got, told, factors)

    for level in (2, 1, 0):
        with jax.named_scope(f"backward_{level}"):
            above = exchange(copies).reshape(NODES, COLS, WIDTH)
            out = backward_level(level, plane1, places, above, forward[level], factors)
            result[level] = out[0]
            if level > 0:
                copies = out[1]

    with jax.named_scope("to_planes"):
        fx = jnp.stack([jnp.stack(solved), jnp.stack(result)], axis=1).reshape(4, 2, 2, 2, COLS, WIDTH)
        fx = lax.all_to_all(fx, "z", 0, 0, tiled=True)
        forward_out, result_out = last_step(core1, fx, swap(fx))
    shape = (1, 2, 1, WIDTH, WIDTH)
    return forward_out.reshape(shape), result_out.reshape(shape)


def solution(mesh):
    wide = Mesh(mesh.devices.reshape(4, 4, 2, 4), ("x", "y", "c", "z"))
    blk = ("x", "y", "c")
    return jax.shard_map(
        on_device,
        mesh=wide,
        in_specs=(
            P("z", None, blk, None, None),
            P("z", None, blk, None, None),
            P("z", None, blk, None, None, None),
            P("z", None, blk, None),
        ),
        out_specs=(P("z", None, blk, None, None), P("z", None, blk, None, None)),
        check_vma=False,
    )
```

```python
import functools

import jax
import jax.numpy as jnp
from jax import lax
from jax.experimental import pallas as pl
from jax.experimental.pallas import tpu as pltpu
from jax.sharding import Mesh, PartitionSpec as P


BF = jnp.bfloat16
F32 = jnp.float32
MIB = 1024 * 1024
LIMIT = 14 * MIB
NODES = 64
CHIPS = 16
WIDTH = 256
FAN = 8
HALF = 128
COLS = 32
UP = [(z, (z + 1) % 4) for z in range(4)]
DOWN = [(z, (z + 3) % 4) for z in range(4)]


SMEM = pl.BlockSpec(memory_space=pltpu.SMEM)
VM = pl.BlockSpec(memory_space=pltpu.VMEM)


def dot_t(a, b):
    return lax.dot_general(a, b, (((1,), (1,)), ((), ())), preferred_element_type=F32)


def dot_n(a, b):
    return lax.dot_general(a, b, (((1,), (0,)), ((), ())), preferred_element_type=F32)


KEEP, SEND, PAT, ROWS = 0, 64, 128, 144


def pack_kernel(core_ref, plane_ref, pat_ref, rhs_ref, out_ref):
    core, plane = core_ref[0], plane_ref[0]
    row = lax.broadcasted_iota(jnp.int32, (ROWS - PAT, WIDTH), 0)
    col = lax.broadcasted_iota(jnp.int32, (ROWS - PAT, WIDTH), 1)
    pat = jnp.zeros((ROWS - PAT, WIDTH), F32)
    for j in range(2):
        for p in range(FAN):
            pat = jnp.where((row == j) & (col == p), pat_ref[j, p].astype(F32), pat)
    for k in range(4):
        out_ref[k, PAT:ROWS] = pat.astype(BF)
    for j in range(2):
        rt = jnp.transpose(rhs_ref[j]).astype(BF)
        for half in range(2):
            at = pl.multiple_of(jnp.where(core == half, KEEP, SEND) + j * COLS, COLS)
            for z in range(4):
                first = half * HALF + z * COLS
                out_ref[jnp.bitwise_and(z - plane + 4, 3), pl.ds(at, COLS)] = rt[first : first + COLS]


def pack(core, plane, pat, rhs):
    return pl.pallas_call(
        pack_kernel,
        out_shape=jax.ShapeDtypeStruct((4, ROWS, WIDTH), BF),
        in_specs=[SMEM, SMEM, SMEM, VM],
        out_specs=VM,
        compiler_params=pltpu.CompilerParams(vmem_limit_bytes=8 * MIB),
        cost_estimate=pl.CostEstimate(flops=0, bytes_accessed=2 * MIB, transcendentals=0),
    )(core, plane, pat, rhs)


ANY = pl.BlockSpec(memory_space=pl.ANY)


def any_specs(count):
    return [ANY] * count


PACKED = FAN + 1


def join_kernel(j, blocks_ref, inv_ref, out_ref, sems):
    copies = [pltpu.make_async_copy(inv_ref.at[j], out_ref.at[FAN], sems.at[0])]
    for k in range(4):
        part = pl.ds(2 * k, 2)
        copies.append(pltpu.make_async_copy(blocks_ref.at[j, part], out_ref.at[part], sems.at[1 + k]))
    for copy in copies:
        copy.start()
    for copy in copies:
        copy.wait()


def join(j, blocks, inverse):
    return pl.pallas_call(
        functools.partial(join_kernel, j),
        in_specs=[ANY, ANY],
        out_specs=VM,
        out_shape=jax.ShapeDtypeStruct((PACKED, WIDTH, WIDTH), BF),
        scratch_shapes=[pltpu.SemaphoreType.DMA((5,))],
        compiler_params=pltpu.CompilerParams(vmem_limit_bytes=3 * MIB),
        cost_estimate=pl.CostEstimate(flops=0, bytes_accessed=3 * MIB, transcendentals=0),
    )(blocks, inverse)


def choose_kernel(chosen, plane_ref, here_ref, else_ref, out_ref, sems):
    for k in range(3):
        part = pl.ds(3 * k, 3)

        @pl.when(plane_ref[0] == chosen)
        def _():
            pltpu.make_async_copy(here_ref.at[part], out_ref.at[part], sems.at[k]).start()

        @pl.when(plane_ref[0] != chosen)
        def _():
            pltpu.make_async_copy(else_ref.at[part], out_ref.at[part], sems.at[k]).start()

    for k in range(3):
        part = pl.ds(3 * k, 3)
        pltpu.make_async_copy(else_ref.at[part], out_ref.at[part], sems.at[k]).wait()


def choose(plane, chosen, here, otherwise):
    return pl.pallas_call(
        functools.partial(choose_kernel, chosen),
        in_specs=[SMEM, ANY, ANY],
        out_specs=VM,
        out_shape=jax.ShapeDtypeStruct((PACKED, WIDTH, WIDTH), BF),
        scratch_shapes=[pltpu.SemaphoreType.DMA((3,))],
        compiler_params=pltpu.CompilerParams(vmem_limit_bytes=3 * MIB),
        cost_estimate=pl.CostEstimate(flops=0, bytes_accessed=3 * MIB, transcendentals=0),
    )(plane, here, otherwise)


WHERE = {
    0: ([0, 2, 4, 5], [1, 4, 5, 3]),
    1: ([5, 0, 2, 4], [3, 1, 6, 7]),
    2: ([4, 5, 0, 2], [7, 3, 1, 6]),
    3: ([2, 6, 7, 0], [6, 7, 3, 1]),
}


def used(level):
    return sorted(set(WHERE[level][0] + WHERE[level][1]))


def on_plane(plane, run):
    for z in range(4):
        pl.when(plane == z)(functools.partial(run, z))


def told_by(plane, level):
    return jnp.bitwise_and(plane - level + 4, 3)


def add_terms(n, at_ref, came, solved, block, acc_ref):
    terms = dot_t(solved, block[:FAN].reshape(FAN * WIDTH, WIDTH))
    for p in range(FAN):
        acc_ref[at_ref[came, n, p]] += terms[:, p * WIDTH : (p + 1) * WIDTH]


def rows_of(told, came, n):
    return told[n // 2][came, pl.ds((KEEP, SEND)[n // 2] + n % 2 * COLS, COLS)]


def inflow_kernel(got_ref, out_ref):
    out_ref[...] = jnp.sum(got_ref[...].astype(F32), axis=0)


def inflow_of(got):
    return pl.pallas_call(
        inflow_kernel,
        in_specs=[VM],
        out_specs=VM,
        out_shape=NODE_F32,
        compiler_params=pltpu.CompilerParams(vmem_limit_bytes=4 * MIB),
        cost_estimate=pl.CostEstimate(flops=MIB, bytes_accessed=MIB, transcendentals=0),
    )(got)


def forward_kernel(level, part, core_ref, plane_ref, at_ref, *rest):
    gots, rest = (rest[:1], rest[1:]) if level else ((), rest)
    before, rest = (rest[:4], rest[4:]) if part == 1 else ((), rest)
    outs = {None: 4, 0: 5, 1: 6}[part]
    told, refs, (f_ref, fb_ref, share_ref, *extra) = rest[:2], rest[2:-outs], rest[-outs:]
    acc_ref = extra[1 if part == 0 else 0]
    names = used(level)
    came = told_by(plane_ref[0], level)

    def block(n, z):
        return refs[len(names) * (n // 2) + names.index(WHERE[level][n % 2][z])]

    def add(nodes, z, block=block):
        solved = {}
        for n in nodes:
            resid = rows_of(told, came, n)
            if level:
                inflow = gots[0][n] if level == 1 else jnp.sum(gots[0][:, n].astype(F32), axis=0)
                resid = (resid.astype(F32) - inflow).astype(BF)
            f = dot_t(resid, block(n, z)[FAN])
            f_ref[n] = f
            solved[n] = f.astype(BF)
            fb_ref[n] = solved[n]
        for n in nodes:
            add_terms(n, at_ref, came, solved[n], block(n, z), acc_ref)

    def run(nodes):
        acc_ref[...] = jnp.zeros_like(acc_ref)
        on_plane(plane_ref[0], functools.partial(add, nodes))
        share_ref[...] = acc_ref[...].astype(BF)

    def finish(n):
        f_ref[:n], fb_ref[:n] = before[0][:n], before[1][:n]
        targets = [at_ref[came, n, p] for p in range(FAN)]
        for t in targets:
            acc_ref[t] = before[3][t]
        on_plane(plane_ref[0], functools.partial(add, (n,)))
        for t in targets:
            share_ref[t] = acc_ref[t].astype(BF)

    def staged():
        buf, sems = extra[1:]

        def copy(n, z):
            return pltpu.make_async_copy(block(n, z), buf.at[n], sems.at[n])

        def start(z):
            for n in range(4):
                copy(n, z).start()

        on_plane(plane_ref[0], start)
        acc_ref[...] = jnp.zeros_like(acc_ref)
        for n in range(4):
            copy(n, 0).wait()
        add((0, 1, 2, 3), 0, lambda n, z: buf.at[n])
        share_ref[...] = acc_ref[...].astype(BF)

    if part is None:
        run((0, 1, 2, 3))
        return

    @pl.when(core_ref[0] == 1)
    def _():
        if part == 0:
            run((0, 1, 2))
            extra[0][...] = acc_ref[...]
        else:
            finish(3)

    if part == 1:

        @pl.when(core_ref[0] == 0)
        def _():
            staged()


STAGE = [pltpu.VMEM((4, PACKED, WIDTH, WIDTH), BF), pltpu.SemaphoreType.DMA((4,))]
NODE_F32 = jax.ShapeDtypeStruct((4, COLS, WIDTH), F32)
NODE_BF = jax.ShapeDtypeStruct((4, COLS, WIDTH), BF)
COPIES = jax.ShapeDtypeStruct((CHIPS, 4, COLS, WIDTH), BF)


def pick(level, factors):
    return [factors[r][k] for r in range(2) for k in used(level)]


def forward_part(level, part, here, at, gots, before, told, blocks):
    shares = jax.ShapeDtypeStruct((NODES, COLS, WIDTH), BF)
    out_shape = (NODE_F32, NODE_BF, shares)
    if part == 0:
        out_shape += (jax.ShapeDtypeStruct((NODES, COLS, WIDTH), F32),)
    return pl.pallas_call(
        functools.partial(forward_kernel, level, part),
        in_specs=[SMEM] * 3 + [VM] * (len(gots) + len(before) + 2 + len(blocks)),
        out_specs=(VM,) * len(out_shape),
        scratch_shapes=[pltpu.VMEM((NODES, COLS, WIDTH), F32)] + (STAGE if part == 1 else []),
        out_shape=out_shape,
        input_output_aliases={3 + len(gots) + 2: 2} if part == 1 else {},
        compiler_params=pltpu.CompilerParams(vmem_limit_bytes=LIMIT),
        cost_estimate=pl.CostEstimate(flops=2 * 36 * COLS * WIDTH**2, bytes_accessed=6 * MIB, transcendentals=0),
    )(*here, at, *gots, *before, *told, *blocks)


def forward_level(level, here, at, gots, told, factors):
    return forward_part(level, None, here, at, gots, (), told, pick(level, factors))


def forward_halves(level, here, at, gots, told, factors):
    early = [factors[0][k] for k in used(level)] + [factors[1][k] for k in used(level) if k < 6]
    before = forward_part(level, 0, here, at, gots, (), told, early)
    return forward_part(level, 1, here, at, gots, before, told, pick(level, factors))


def top_kernel(plane_ref, got_ref, own_told, other_told, *rest):
    refs, (fb_ref, sol_ref, copies_ref) = rest[:-3], rest[-3:]
    names = used(3)
    came = told_by(plane_ref[0], 3)
    resids = []
    for n in range(4):
        inflow = jnp.sum(got_ref[:, n].astype(F32), axis=0)
        resids.append((rows_of((own_told, other_told), came, n).astype(F32) - inflow).astype(BF))

    def run(z):
        invs = [refs[len(names) * (n // 2) + names.index(WHERE[3][n % 2][z])].at[FAN] for n in range(4)]
        solved = []
        for n in range(4):
            solved.append(dot_t(resids[n], invs[n][...]).astype(BF))
            fb_ref[n] = solved[n]
        for n in range(4):
            sol = dot_n(solved[n], invs[n][...]).astype(BF)
            sol_ref[n] = sol
            for k in range(CHIPS):
                copies_ref[k, n] = sol

    on_plane(plane_ref[0], run)


def top_level(plane, got, told, factors):
    blocks = pick(3, factors)
    return pl.pallas_call(
        top_kernel,
        in_specs=[SMEM] + [VM] * (3 + len(blocks)),
        out_specs=(VM, VM, VM),
        out_shape=(NODE_BF, NODE_BF, COPIES),
        compiler_params=pltpu.CompilerParams(vmem_limit_bytes=LIMIT),
        cost_estimate=pl.CostEstimate(flops=2 * 8 * COLS * WIDTH**2, bytes_accessed=3 * MIB, transcendentals=0),
    )(plane, got, *told, *blocks)


def backward_kernel(level, plane_ref, at_ref, above_ref, f_ref, *rest):
    names = used(level)
    refs, outs = rest[: 2 * len(names)], rest[2 * len(names) :]
    came = told_by(plane_ref[0], level)

    def run(z):
        blocks = [refs[len(names) * (n // 2) + names.index(WHERE[level][n % 2][z])] for n in range(4)]
        uppers = []
        for n in range(4):
            picked = jnp.concatenate([above_ref[at_ref[came, n, p]] for p in range(FAN)], axis=1)
            back = dot_n(picked, blocks[n][:FAN].reshape(FAN * WIDTH, WIDTH))
            uppers.append((f_ref[n] - back).astype(BF))
        for n in range(4):
            sol = dot_n(uppers[n], blocks[n][FAN]).astype(BF)
            outs[0][n] = sol
            if level:
                for k in range(CHIPS):
                    outs[1][k, n] = sol

    on_plane(plane_ref[0], run)


def backward_level(level, plane, at, above, f, factors):
    blocks = pick(level, factors)
    out_shape = (NODE_BF, COPIES) if level else (NODE_BF,)
    return pl.pallas_call(
        functools.partial(backward_kernel, level),
        in_specs=[SMEM, SMEM] + [VM] * (2 + len(blocks)),
        out_specs=(VM,) * len(out_shape),
        out_shape=out_shape,
        compiler_params=pltpu.CompilerParams(vmem_limit_bytes=LIMIT),
        cost_estimate=pl.CostEstimate(flops=2 * 36 * COLS * WIDTH**2, bytes_accessed=6 * MIB, transcendentals=0),
    )(plane, at, above, f, *blocks)


def last_kernel(core_ref, own_ref, other_ref, forward_ref, result_ref):
    core = core_ref[0]
    for k, out_ref in enumerate((forward_ref, result_ref)):
        for j in range(2):
            own = jnp.concatenate([own_ref[z, k, 0, j] for z in range(4)], axis=0).astype(F32)
            other = jnp.concatenate([other_ref[z, k, 1, j] for z in range(4)], axis=0).astype(F32)
            low, high = jnp.where(core == 0, own, other), jnp.where(core == 0, other, own)
            out_ref[j] = jnp.transpose(jnp.concatenate([low, high], axis=0))


def last_step(core, own, other):
    return pl.pallas_call(
        last_kernel,
        out_shape=(jax.ShapeDtypeStruct((2, WIDTH, WIDTH), F32),) * 2,
        in_specs=[SMEM, VM, VM],
        out_specs=(VM, VM),
        compiler_params=pltpu.CompilerParams(vmem_limit_bytes=8 * MIB),
        cost_estimate=pl.CostEstimate(flops=0, bytes_accessed=2 * MIB, transcendentals=0),
    )(core, own, other)


def swap(value):
    return lax.ppermute(value, "c", [(0, 1), (1, 0)])


def exchange(value):
    return lax.all_to_all(value.reshape(CHIPS, 4, COLS, WIDTH), ("y", "x"), 0, 0, tiled=True)


def on_device(rhs, inverses, blocks, pattern):
    core = lax.axis_index("c").astype(jnp.int32)
    plane = lax.axis_index("z").astype(jnp.int32)
    core1, plane1 = core.reshape(1), plane.reshape(1)
    factor = blocks.reshape(2, FAN, WIDTH, WIDTH)
    inverse = inverses.reshape(2, WIDTH, WIDTH)

    with jax.named_scope("tell_planes"):
        message = pack(core1, plane1, pattern.reshape(2, FAN), rhs.reshape(2, WIDTH, WIDTH))
        told = [message[0]]
        for k in range(1, 4):
            told.append(lax.ppermute(message[k], "z", [(z, (z + k) % 4) for z in range(4)]))

    with jax.named_scope("factor_step_1"):
        own_a, own_b = join(0, factor, inverse), join(1, factor, inverse)
        own_a, own_b, told = lax.optimization_barrier((own_a, own_b, told))
        up_1 = lax.ppermute(own_a, "z", UP)
        down_1 = lax.ppermute(own_b, "z", DOWN)
        near_a, near_b = swap(own_a), swap(own_b)

    with jax.named_scope("tell_planes"):
        told = jnp.stack(told)
        told = (told, swap(told))
        targets = jnp.concatenate([t[:, PAT : PAT + 2, :FAN] for t in told], axis=1).astype(jnp.int32)
        targets = jnp.clip(targets, 0, NODES - 1)
        chip = targets % 8 // 2 * 4 + targets % 32 // 8
        places = chip * 4 + jnp.bitwise_xor(targets % 2, core) * 2 + targets // 32

    with jax.named_scope("factor_step_2"):
        up_2 = lax.ppermute(choose(plane1, 0, own_b, up_1), "z", UP)
        down_2 = lax.ppermute(choose(plane1, 3, down_1, own_a), "z", DOWN)
        up_3 = choose(plane1, 0, up_1, own_b)
        down_3 = choose(plane1, 3, own_a, down_1)
        near = (near_a, near_b, swap(up_1), swap(down_1))
        up_2, down_2, up_3, down_3, told, places, near = lax.optimization_barrier(
            (up_2, down_2, up_3, down_3, told, places, near)
        )
        near += (swap(up_2), swap(down_2))
    with jax.named_scope("factor_step_3"):
        up_3 = lax.ppermute(up_3, "z", UP)
        down_3 = lax.ppermute(down_3, "z", DOWN)

    factors = ([own_a, own_b, up_1, down_1, up_2, down_2], list(near))
    forward = [None] * 3
    solved = [None] * 4
    gots = ()
    for level in range(3):
        with jax.named_scope(f"forward_{level}"):
            solve = forward_halves if level == 1 else forward_level
            forward[level], solved[level], share = solve(level, (core1, plane1), places, gots, told, factors)
            got = exchange(share)
        if level == 0:
            with jax.named_scope("factor_step_3"):
                up_3, down_3, got = lax.optimization_barrier((up_3, down_3, inflow_of(got)))
                factors[0].extend([up_3, down_3])
                factors[1].extend([swap(up_3), swap(down_3)])
        gots = (got,)
    result = [None] * 4
    with jax.named_scope("top"):
        solved[3], result[3], copies = top_level(plane1, got, told, factors)

    for level in (2, 1, 0):
        with jax.named_scope(f"backward_{level}"):
            above = exchange(copies).reshape(NODES, COLS, WIDTH)
            out = backward_level(level, plane1, places, above, forward[level], factors)
            result[level] = out[0]
            if level > 0:
                copies = out[1]

    with jax.named_scope("to_planes"):
        fx = jnp.stack([jnp.stack(solved), jnp.stack(result)], axis=1).reshape(4, 2, 2, 2, COLS, WIDTH)
        fx = lax.all_to_all(fx, "z", 0, 0, tiled=True)
        forward_out, result_out = last_step(core1, fx, swap(fx))
    shape = (1, 2, 1, WIDTH, WIDTH)
    return forward_out.reshape(shape), result_out.reshape(shape)


def solution(mesh):
    wide = Mesh(mesh.devices.reshape(4, 4, 2, 4), ("x", "y", "c", "z"))
    blk = ("x", "y", "c")
    return jax.shard_map(
        on_device,
        mesh=wide,
        in_specs=(
            P("z", None, blk, None, None),
            P("z", None, blk, None, None),
            P("z", None, blk, None, None, None),
            P("z", None, blk, None),
        ),
        out_specs=(P("z", None, blk, None, None), P("z", None, blk, None, None)),
        check_vma=False,
    )
```

```python
import functools

import jax
import jax.numpy as jnp
from jax import lax
from jax.experimental import pallas as pl
from jax.experimental.pallas import tpu as pltpu
from jax.sharding import Mesh, PartitionSpec as P


BF = jnp.bfloat16
F32 = jnp.float32
MIB = 1024 * 1024
LIMIT = 14 * MIB
NODES = 64
CHIPS = 16
WIDTH = 256
FAN = 8
HALF = 128
COLS = 32
UP = [(z, (z + 1) % 4) for z in range(4)]
DOWN = [(z, (z + 3) % 4) for z in range(4)]


SMEM = pl.BlockSpec(memory_space=pltpu.SMEM)
VM = pl.BlockSpec(memory_space=pltpu.VMEM)


def dot_t(a, b):
    return lax.dot_general(a, b, (((1,), (1,)), ((), ())), preferred_element_type=F32)


def dot_n(a, b):
    return lax.dot_general(a, b, (((1,), (0,)), ((), ())), preferred_element_type=F32)


KEEP, SEND, PAT, ROWS = 0, 64, 128, 144


def pack_kernel(core_ref, plane_ref, pat_ref, rhs_ref, out_ref):
    core, plane = core_ref[0], plane_ref[0]
    row = lax.broadcasted_iota(jnp.int32, (ROWS - PAT, WIDTH), 0)
    col = lax.broadcasted_iota(jnp.int32, (ROWS - PAT, WIDTH), 1)
    pat = jnp.zeros((ROWS - PAT, WIDTH), F32)
    for j in range(2):
        for p in range(FAN):
            pat = jnp.where((row == j) & (col == p), pat_ref[j, p].astype(F32), pat)
    for k in range(4):
        out_ref[k, PAT:ROWS] = pat.astype(BF)
    for j in range(2):
        rt = jnp.transpose(rhs_ref[j]).astype(BF)
        for half in range(2):
            at = pl.multiple_of(jnp.where(core == half, KEEP, SEND) + j * COLS, COLS)
            for z in range(4):
                first = half * HALF + z * COLS
                out_ref[jnp.bitwise_and(z - plane + 4, 3), pl.ds(at, COLS)] = rt[first : first + COLS]


def pack(core, plane, pat, rhs):
    return pl.pallas_call(
        pack_kernel,
        out_shape=jax.ShapeDtypeStruct((4, ROWS, WIDTH), BF),
        in_specs=[SMEM, SMEM, SMEM, VM],
        out_specs=VM,
        compiler_params=pltpu.CompilerParams(vmem_limit_bytes=8 * MIB),
        cost_estimate=pl.CostEstimate(flops=0, bytes_accessed=2 * MIB, transcendentals=0),
    )(core, plane, pat, rhs)


ANY = pl.BlockSpec(memory_space=pl.ANY)


def any_specs(count):
    return [ANY] * count


PACKED = FAN + 1


def join_kernel(j, blocks_ref, inv_ref, out_ref, sems):
    copies = [pltpu.make_async_copy(inv_ref.at[j], out_ref.at[FAN], sems.at[0])]
    for k in range(4):
        part = pl.ds(2 * k, 2)
        copies.append(pltpu.make_async_copy(blocks_ref.at[j, part], out_ref.at[part], sems.at[1 + k]))
    for copy in copies:
        copy.start()
    for copy in copies:
        copy.wait()


def join(j, blocks, inverse):
    return pl.pallas_call(
        functools.partial(join_kernel, j),
        in_specs=[ANY, ANY],
        out_specs=VM,
        out_shape=jax.ShapeDtypeStruct((PACKED, WIDTH, WIDTH), BF),
        scratch_shapes=[pltpu.SemaphoreType.DMA((5,))],
        compiler_params=pltpu.CompilerParams(vmem_limit_bytes=3 * MIB),
        cost_estimate=pl.CostEstimate(flops=0, bytes_accessed=3 * MIB, transcendentals=0),
    )(blocks, inverse)


def choose_kernel(chosen, plane_ref, here_ref, else_ref, out_ref, sems):
    for k in range(3):
        part = pl.ds(3 * k, 3)

        @pl.when(plane_ref[0] == chosen)
        def _():
            pltpu.make_async_copy(here_ref.at[part], out_ref.at[part], sems.at[k]).start()

        @pl.when(plane_ref[0] != chosen)
        def _():
            pltpu.make_async_copy(else_ref.at[part], out_ref.at[part], sems.at[k]).start()

    for k in range(3):
        part = pl.ds(3 * k, 3)
        pltpu.make_async_copy(else_ref.at[part], out_ref.at[part], sems.at[k]).wait()


def choose(plane, chosen, here, otherwise):
    return pl.pallas_call(
        functools.partial(choose_kernel, chosen),
        in_specs=[SMEM, ANY, ANY],
        out_specs=VM,
        out_shape=jax.ShapeDtypeStruct((PACKED, WIDTH, WIDTH), BF),
        scratch_shapes=[pltpu.SemaphoreType.DMA((3,))],
        compiler_params=pltpu.CompilerParams(vmem_limit_bytes=3 * MIB),
        cost_estimate=pl.CostEstimate(flops=0, bytes_accessed=3 * MIB, transcendentals=0),
    )(plane, here, otherwise)


WHERE = {
    0: ([0, 2, 4, 5], [1, 4, 5, 3]),
    1: ([5, 0, 2, 4], [3, 1, 6, 7]),
    2: ([4, 5, 0, 2], [7, 3, 1, 6]),
    3: ([2, 6, 7, 0], [6, 7, 3, 1]),
}


def used(level):
    return sorted(set(WHERE[level][0] + WHERE[level][1]))


def on_plane(plane, run):
    for z in range(4):
        pl.when(plane == z)(functools.partial(run, z))


def told_by(plane, level):
    return jnp.bitwise_and(plane - level + 4, 3)


def add_terms(n, at_ref, came, solved, block, acc_ref):
    terms = dot_t(solved, block[:FAN].reshape(FAN * WIDTH, WIDTH))
    for p in range(FAN):
        acc_ref[at_ref[came, n, p]] += terms[:, p * WIDTH : (p + 1) * WIDTH]


def rows_of(told, came, n):
    return told[n // 2][came, pl.ds((KEEP, SEND)[n // 2] + n % 2 * COLS, COLS)]


def inflow_kernel(got_ref, out_ref):
    out_ref[...] = jnp.sum(got_ref[...].astype(F32), axis=0)


def inflow_of(got):
    return pl.pallas_call(
        inflow_kernel,
        in_specs=[VM],
        out_specs=VM,
        out_shape=NODE_F32,
        compiler_params=pltpu.CompilerParams(vmem_limit_bytes=4 * MIB),
        cost_estimate=pl.CostEstimate(flops=MIB, bytes_accessed=MIB, transcendentals=0),
    )(got)


def forward_kernel(level, part, core_ref, plane_ref, at_ref, *rest):
    gots, rest = (rest[:1], rest[1:]) if level else ((), rest)
    before, rest = (rest[:4], rest[4:]) if part == 1 else ((), rest)
    outs = {None: 4, 0: 5, 1: 6}[part]
    told, refs, (f_ref, fb_ref, share_ref, *extra) = rest[:2], rest[2:-outs], rest[-outs:]
    acc_ref = extra[1 if part == 0 else 0]
    names = used(level)
    came = told_by(plane_ref[0], level)

    def block(n, z):
        return refs[len(names) * (n // 2) + names.index(WHERE[level][n % 2][z])]

    def add(nodes, z, block=block):
        solved = {}
        for n in nodes:
            resid = rows_of(told, came, n)
            if level:
                inflow = gots[0][n] if level == 1 else jnp.sum(gots[0][:, n].astype(F32), axis=0)
                resid = (resid.astype(F32) - inflow).astype(BF)
            f = dot_t(resid, block(n, z)[FAN])
            f_ref[n] = f
            solved[n] = f.astype(BF)
            fb_ref[n] = solved[n]
        for n in nodes:
            add_terms(n, at_ref, came, solved[n], block(n, z), acc_ref)

    def run(nodes):
        acc_ref[...] = jnp.zeros_like(acc_ref)
        on_plane(plane_ref[0], functools.partial(add, nodes))
        share_ref[...] = acc_ref[...].astype(BF)

    def finish(n):
        f_ref[:n], fb_ref[:n] = before[0][:n], before[1][:n]
        targets = [at_ref[came, n, p] for p in range(FAN)]
        for t in targets:
            acc_ref[t] = before[3][t]
        on_plane(plane_ref[0], functools.partial(add, (n,)))
        for t in targets:
            share_ref[t] = acc_ref[t].astype(BF)

    def staged():
        buf, sems = extra[1:]

        def copy(n, z):
            return pltpu.make_async_copy(block(n, z), buf.at[n], sems.at[n])

        def start(z):
            for n in range(4):
                copy(n, z).start()

        on_plane(plane_ref[0], start)
        acc_ref[...] = jnp.zeros_like(acc_ref)
        for n in range(4):
            copy(n, 0).wait()
        add((0, 1, 2, 3), 0, lambda n, z: buf.at[n])
        share_ref[...] = acc_ref[...].astype(BF)

    if part is None:
        run((0, 1, 2, 3))
        return

    @pl.when(core_ref[0] == 1)
    def _():
        if part == 0:
            run((0, 1, 2))
            extra[0][...] = acc_ref[...]
        else:
            finish(3)

    if part == 1:

        @pl.when(core_ref[0] == 0)
        def _():
            staged()


STAGE = [pltpu.VMEM((4, PACKED, WIDTH, WIDTH), BF), pltpu.SemaphoreType.DMA((4,))]
NODE_F32 = jax.ShapeDtypeStruct((4, COLS, WIDTH), F32)
NODE_BF = jax.ShapeDtypeStruct((4, COLS, WIDTH), BF)
COPIES = jax.ShapeDtypeStruct((CHIPS, 4, COLS, WIDTH), BF)


def pick(level, factors):
    return [factors[r][k] for r in range(2) for k in used(level)]


def forward_part(level, part, here, at, gots, before, told, blocks):
    shares = jax.ShapeDtypeStruct((NODES, COLS, WIDTH), BF)
    out_shape = (NODE_F32, NODE_BF, shares)
    if part == 0:
        out_shape += (jax.ShapeDtypeStruct((NODES, COLS, WIDTH), F32),)
    return pl.pallas_call(
        functools.partial(forward_kernel, level, part),
        in_specs=[SMEM] * 3 + [VM] * (len(gots) + len(before) + 2 + len(blocks)),
        out_specs=(VM,) * len(out_shape),
        scratch_shapes=[pltpu.VMEM((NODES, COLS, WIDTH), F32)] + (STAGE if part == 1 else []),
        out_shape=out_shape,
        input_output_aliases={3 + len(gots) + 2: 2} if part == 1 else {},
        compiler_params=pltpu.CompilerParams(vmem_limit_bytes=LIMIT),
        cost_estimate=pl.CostEstimate(flops=2 * 36 * COLS * WIDTH**2, bytes_accessed=6 * MIB, transcendentals=0),
    )(*here, at, *gots, *before, *told, *blocks)


def forward_level(level, here, at, gots, told, factors):
    return forward_part(level, None, here, at, gots, (), told, pick(level, factors))


def forward_halves(level, here, at, gots, told, factors):
    early = [factors[0][k] for k in used(level)] + [factors[1][k] for k in used(level) if k < 6]
    before = forward_part(level, 0, here, at, gots, (), told, early)
    return forward_part(level, 1, here, at, gots, before, told, pick(level, factors))


def top_kernel(plane_ref, got_ref, own_told, other_told, *rest):
    refs, (fb_ref, sol_ref, copies_ref) = rest[:-3], rest[-3:]
    names = used(3)
    came = told_by(plane_ref[0], 3)
    resids = []
    for n in range(4):
        inflow = jnp.sum(got_ref[:, n].astype(F32), axis=0)
        resids.append((rows_of((own_told, other_told), came, n).astype(F32) - inflow).astype(BF))

    def run(z):
        invs = [refs[len(names) * (n // 2) + names.index(WHERE[3][n % 2][z])].at[FAN] for n in range(4)]
        solved = []
        for n in range(4):
            solved.append(dot_t(resids[n], invs[n][...]).astype(BF))
            fb_ref[n] = solved[n]
        for n in range(4):
            sol = dot_n(solved[n], invs[n][...]).astype(BF)
            sol_ref[n] = sol
            for k in range(CHIPS):
                copies_ref[k, n] = sol

    on_plane(plane_ref[0], run)


def top_level(plane, got, told, factors):
    blocks = pick(3, factors)
    return pl.pallas_call(
        top_kernel,
        in_specs=[SMEM] + [VM] * (3 + len(blocks)),
        out_specs=(VM, VM, VM),
        out_shape=(NODE_BF, NODE_BF, COPIES),
        compiler_params=pltpu.CompilerParams(vmem_limit_bytes=LIMIT),
        cost_estimate=pl.CostEstimate(flops=2 * 8 * COLS * WIDTH**2, bytes_accessed=3 * MIB, transcendentals=0),
    )(plane, got, *told, *blocks)


def backward_kernel(level, plane_ref, at_ref, above_ref, f_ref, *rest):
    names = used(level)
    refs, outs = rest[: 2 * len(names)], rest[2 * len(names) :]
    came = told_by(plane_ref[0], level)

    def run(z):
        blocks = [refs[len(names) * (n // 2) + names.index(WHERE[level][n % 2][z])] for n in range(4)]
        uppers = []
        for n in range(4):
            picked = jnp.concatenate([above_ref[at_ref[came, n, p]] for p in range(FAN)], axis=1)
            back = dot_n(picked, blocks[n][:FAN].reshape(FAN * WIDTH, WIDTH))
            uppers.append((f_ref[n] - back).astype(BF))
        for n in range(4):
            sol = dot_n(uppers[n], blocks[n][FAN]).astype(BF)
            outs[0][n] = sol
            if level:
                for k in range(CHIPS):
                    outs[1][k, n] = sol

    on_plane(plane_ref[0], run)


def backward_level(level, plane, at, above, f, factors):
    blocks = pick(level, factors)
    out_shape = (NODE_BF, COPIES) if level else (NODE_BF,)
    return pl.pallas_call(
        functools.partial(backward_kernel, level),
        in_specs=[SMEM, SMEM] + [VM] * (2 + len(blocks)),
        out_specs=(VM,) * len(out_shape),
        out_shape=out_shape,
        compiler_params=pltpu.CompilerParams(vmem_limit_bytes=LIMIT),
        cost_estimate=pl.CostEstimate(flops=2 * 36 * COLS * WIDTH**2, bytes_accessed=6 * MIB, transcendentals=0),
    )(plane, at, above, f, *blocks)


def last_kernel(core_ref, own_ref, other_ref, forward_ref, result_ref):
    core = core_ref[0]
    for k, out_ref in enumerate((forward_ref, result_ref)):
        for j in range(2):
            own = jnp.concatenate([own_ref[z, k, 0, j] for z in range(4)], axis=0).astype(F32)
            other = jnp.concatenate([other_ref[z, k, j] for z in range(4)], axis=0).astype(F32)
            low, high = jnp.where(core == 0, own, other), jnp.where(core == 0, other, own)
            out_ref[j] = jnp.transpose(jnp.concatenate([low, high], axis=0))


def last_step(core, own, other):
    return pl.pallas_call(
        last_kernel,
        out_shape=(jax.ShapeDtypeStruct((2, WIDTH, WIDTH), F32),) * 2,
        in_specs=[SMEM, VM, VM],
        out_specs=(VM, VM),
        compiler_params=pltpu.CompilerParams(vmem_limit_bytes=8 * MIB),
        cost_estimate=pl.CostEstimate(flops=0, bytes_accessed=2 * MIB, transcendentals=0),
    )(core, own, other)


def swap(value):
    return lax.ppermute(value, "c", [(0, 1), (1, 0)])


def exchange(value):
    return lax.all_to_all(value.reshape(CHIPS, 4, COLS, WIDTH), ("y", "x"), 0, 0, tiled=True)


def on_device(rhs, inverses, blocks, pattern):
    core = lax.axis_index("c").astype(jnp.int32)
    plane = lax.axis_index("z").astype(jnp.int32)
    core1, plane1 = core.reshape(1), plane.reshape(1)
    factor = blocks.reshape(2, FAN, WIDTH, WIDTH)
    inverse = inverses.reshape(2, WIDTH, WIDTH)

    with jax.named_scope("tell_planes"):
        message = pack(core1, plane1, pattern.reshape(2, FAN), rhs.reshape(2, WIDTH, WIDTH))
        told = [message[0]]
        for k in range(1, 4):
            told.append(lax.ppermute(message[k], "z", [(z, (z + k) % 4) for z in range(4)]))

    with jax.named_scope("factor_step_1"):
        own_a, own_b = join(0, factor, inverse), join(1, factor, inverse)
        own_a, own_b, told = lax.optimization_barrier((own_a, own_b, told))
        up_1 = lax.ppermute(own_a, "z", UP)
        down_1 = lax.ppermute(own_b, "z", DOWN)
        near_a, near_b = swap(own_a), swap(own_b)

    with jax.named_scope("tell_planes"):
        told = jnp.stack(told)
        told = (told, swap(told))
        targets = jnp.concatenate([t[:, PAT : PAT + 2, :FAN] for t in told], axis=1).astype(jnp.int32)
        targets = jnp.clip(targets, 0, NODES - 1)
        chip = targets % 8 // 2 * 4 + targets % 32 // 8
        places = chip * 4 + jnp.bitwise_xor(targets % 2, core) * 2 + targets // 32

    with jax.named_scope("factor_step_2"):
        up_2 = lax.ppermute(choose(plane1, 0, own_b, up_1), "z", UP)
        down_2 = lax.ppermute(choose(plane1, 3, down_1, own_a), "z", DOWN)
        up_3 = choose(plane1, 0, up_1, own_b)
        down_3 = choose(plane1, 3, own_a, down_1)
        near = (near_a, near_b, swap(up_1), swap(down_1))
        up_2, down_2, up_3, down_3, told, places, near = lax.optimization_barrier(
            (up_2, down_2, up_3, down_3, told, places, near)
        )
        near += (swap(up_2), swap(down_2))
    with jax.named_scope("factor_step_3"):
        up_3 = lax.ppermute(up_3, "z", UP)
        down_3 = lax.ppermute(down_3, "z", DOWN)

    factors = ([own_a, own_b, up_1, down_1, up_2, down_2], list(near))
    forward = [None] * 3
    solved = [None] * 4
    gots = ()
    for level in range(3):
        with jax.named_scope(f"forward_{level}"):
            solve = forward_halves if level == 1 else forward_level
            forward[level], solved[level], share = solve(level, (core1, plane1), places, gots, told, factors)
            got = exchange(share)
        if level == 0:
            with jax.named_scope("factor_step_3"):
                up_3, down_3, got = lax.optimization_barrier((up_3, down_3, inflow_of(got)))
                factors[0].extend([up_3, down_3])
                factors[1].extend([swap(up_3), swap(down_3)])
        gots = (got,)
    result = [None] * 4
    with jax.named_scope("top"):
        solved[3], result[3], copies = top_level(plane1, got, told, factors)

    for level in (2, 1, 0):
        with jax.named_scope(f"backward_{level}"):
            above = exchange(copies).reshape(NODES, COLS, WIDTH)
            out = backward_level(level, plane1, places, above, forward[level], factors)
            result[level] = out[0]
            if level > 0:
                copies = out[1]

    with jax.named_scope("to_planes"):
        fx = jnp.stack([jnp.stack(solved), jnp.stack(result)], axis=1).reshape(4, 2, 2, 2, COLS, WIDTH)
        fx = lax.all_to_all(fx, "z", 0, 0, tiled=True)
        forward_out, result_out = last_step(core1, fx, swap(fx[:, :, 1]))
    shape = (1, 2, 1, WIDTH, WIDTH)
    return forward_out.reshape(shape), result_out.reshape(shape)


def solution(mesh):
    wide = Mesh(mesh.devices.reshape(4, 4, 2, 4), ("x", "y", "c", "z"))
    blk = ("x", "y", "c")
    return jax.shard_map(
        on_device,
        mesh=wide,
        in_specs=(
            P("z", None, blk, None, None),
            P("z", None, blk, None, None),
            P("z", None, blk, None, None, None),
            P("z", None, blk, None),
        ),
        out_specs=(P("z", None, blk, None, None), P("z", None, blk, None, None)),
        check_vma=False,
    )
```

```python
import functools

import jax
import jax.numpy as jnp
from jax import lax
from jax.experimental import pallas as pl
from jax.experimental.pallas import tpu as pltpu
from jax.sharding import Mesh, PartitionSpec as P


BF = jnp.bfloat16
F32 = jnp.float32
MIB = 1024 * 1024
LIMIT = 14 * MIB
NODES = 64
CHIPS = 16
WIDTH = 256
FAN = 8
HALF = 128
COLS = 32
UP = [(z, (z + 1) % 4) for z in range(4)]
DOWN = [(z, (z + 3) % 4) for z in range(4)]


SMEM = pl.BlockSpec(memory_space=pltpu.SMEM)
VM = pl.BlockSpec(memory_space=pltpu.VMEM)


def dot_t(a, b):
    return lax.dot_general(a, b, (((1,), (1,)), ((), ())), preferred_element_type=F32)


def dot_n(a, b):
    return lax.dot_general(a, b, (((1,), (0,)), ((), ())), preferred_element_type=F32)


KEEP, SEND, PAT, ROWS = 0, 64, 128, 144


def pack_kernel(core_ref, plane_ref, pat_ref, rhs_ref, out_ref):
    core, plane = core_ref[0], plane_ref[0]
    row = lax.broadcasted_iota(jnp.int32, (ROWS - PAT, WIDTH), 0)
    col = lax.broadcasted_iota(jnp.int32, (ROWS - PAT, WIDTH), 1)
    pat = jnp.zeros((ROWS - PAT, WIDTH), F32)
    for j in range(2):
        for p in range(FAN):
            pat = jnp.where((row == j) & (col == p), pat_ref[j, p].astype(F32), pat)
    for k in range(4):
        out_ref[k, PAT:ROWS] = pat.astype(BF)
    for j in range(2):
        rt = jnp.transpose(rhs_ref[j]).astype(BF)
        for half in range(2):
            at = pl.multiple_of(jnp.where(core == half, KEEP, SEND) + j * COLS, COLS)
            for z in range(4):
                first = half * HALF + z * COLS
                out_ref[jnp.bitwise_and(z - plane + 4, 3), pl.ds(at, COLS)] = rt[first : first + COLS]


def pack(core, plane, pat, rhs):
    return pl.pallas_call(
        pack_kernel,
        out_shape=jax.ShapeDtypeStruct((4, ROWS, WIDTH), BF),
        in_specs=[SMEM, SMEM, SMEM, VM],
        out_specs=VM,
        compiler_params=pltpu.CompilerParams(vmem_limit_bytes=8 * MIB),
        cost_estimate=pl.CostEstimate(flops=0, bytes_accessed=2 * MIB, transcendentals=0),
    )(core, plane, pat, rhs)


ANY = pl.BlockSpec(memory_space=pl.ANY)


def any_specs(count):
    return [ANY] * count


PACKED = FAN + 1


def join_kernel(j, blocks_ref, inv_ref, out_ref, sems):
    copies = [pltpu.make_async_copy(inv_ref.at[j], out_ref.at[FAN], sems.at[0])]
    for k in range(4):
        part = pl.ds(2 * k, 2)
        copies.append(pltpu.make_async_copy(blocks_ref.at[j, part], out_ref.at[part], sems.at[1 + k]))
    for copy in copies:
        copy.start()
    for copy in copies:
        copy.wait()


def join(j, blocks, inverse):
    return pl.pallas_call(
        functools.partial(join_kernel, j),
        in_specs=[ANY, ANY],
        out_specs=VM,
        out_shape=jax.ShapeDtypeStruct((PACKED, WIDTH, WIDTH), BF),
        scratch_shapes=[pltpu.SemaphoreType.DMA((5,))],
        compiler_params=pltpu.CompilerParams(vmem_limit_bytes=3 * MIB),
        cost_estimate=pl.CostEstimate(flops=0, bytes_accessed=3 * MIB, transcendentals=0),
    )(blocks, inverse)


def choose_kernel(chosen, plane_ref, here_ref, else_ref, out_ref, sems):
    for k in range(3):
        part = pl.ds(3 * k, 3)

        @pl.when(plane_ref[0] == chosen)
        def _():
            pltpu.make_async_copy(here_ref.at[part], out_ref.at[part], sems.at[k]).start()

        @pl.when(plane_ref[0] != chosen)
        def _():
            pltpu.make_async_copy(else_ref.at[part], out_ref.at[part], sems.at[k]).start()

    for k in range(3):
        part = pl.ds(3 * k, 3)
        pltpu.make_async_copy(else_ref.at[part], out_ref.at[part], sems.at[k]).wait()


def choose(plane, chosen, here, otherwise):
    return pl.pallas_call(
        functools.partial(choose_kernel, chosen),
        in_specs=[SMEM, ANY, ANY],
        out_specs=VM,
        out_shape=jax.ShapeDtypeStruct((PACKED, WIDTH, WIDTH), BF),
        scratch_shapes=[pltpu.SemaphoreType.DMA((3,))],
        compiler_params=pltpu.CompilerParams(vmem_limit_bytes=3 * MIB),
        cost_estimate=pl.CostEstimate(flops=0, bytes_accessed=3 * MIB, transcendentals=0),
    )(plane, here, otherwise)


WHERE = {
    0: ([0, 2, 4, 5], [1, 4, 5, 3]),
    1: ([5, 0, 2, 4], [3, 1, 6, 7]),
    2: ([4, 5, 0, 2], [7, 3, 1, 6]),
    3: ([2, 6, 7, 0], [6, 7, 3, 1]),
}


def used(level):
    return sorted(set(WHERE[level][0] + WHERE[level][1]))


def on_plane(plane, run):
    for z in range(4):
        pl.when(plane == z)(functools.partial(run, z))


def told_by(plane, level):
    return jnp.bitwise_and(plane - level + 4, 3)


def add_terms(n, at_ref, came, solved, block, acc_ref):
    terms = dot_t(solved, block[:FAN].reshape(FAN * WIDTH, WIDTH))
    for p in range(FAN):
        acc_ref[at_ref[came, n, p]] += terms[:, p * WIDTH : (p + 1) * WIDTH]


def rows_of(told, came, n):
    return told[n // 2][came, pl.ds((KEEP, SEND)[n // 2] + n % 2 * COLS, COLS)]


def inflow_kernel(got_ref, out_ref):
    out_ref[...] = jnp.sum(got_ref[...].astype(F32), axis=0)


def inflow_of(got):
    return pl.pallas_call(
        inflow_kernel,
        in_specs=[VM],
        out_specs=VM,
        out_shape=NODE_F32,
        compiler_params=pltpu.CompilerParams(vmem_limit_bytes=4 * MIB),
        cost_estimate=pl.CostEstimate(flops=MIB, bytes_accessed=MIB, transcendentals=0),
    )(got)


def forward_kernel(level, part, core_ref, plane_ref, at_ref, *rest):
    gots, rest = (rest[:1], rest[1:]) if level else ((), rest)
    before, rest = (rest[:4], rest[4:]) if part == 1 else ((), rest)
    outs = {None: 4, 0: 5, 1: 6}[part]
    told, refs, (f_ref, fb_ref, share_ref, *extra) = rest[:2], rest[2:-outs], rest[-outs:]
    acc_ref = extra[1 if part == 0 else 0]
    names = used(level)
    came = told_by(plane_ref[0], level)

    def block(n, z):
        return refs[len(names) * (n // 2) + names.index(WHERE[level][n % 2][z])]

    def add(nodes, z, block=block):
        solved = {}
        for n in nodes:
            resid = rows_of(told, came, n)
            if level:
                inflow = gots[0][n] if level == 1 else jnp.sum(gots[0][:, n].astype(F32), axis=0)
                resid = (resid.astype(F32) - inflow).astype(BF)
            f = dot_t(resid, block(n, z)[FAN])
            f_ref[n] = f
            solved[n] = f.astype(BF)
            fb_ref[n] = solved[n]
        for n in nodes:
            add_terms(n, at_ref, came, solved[n], block(n, z), acc_ref)

    def run(nodes):
        acc_ref[...] = jnp.zeros_like(acc_ref)
        on_plane(plane_ref[0], functools.partial(add, nodes))
        share_ref[...] = acc_ref[...].astype(BF)

    def finish(n):
        f_ref[:n], fb_ref[:n] = before[0][:n], before[1][:n]
        targets = [at_ref[came, n, p] for p in range(FAN)]
        for t in targets:
            acc_ref[t] = before[3][t]
        on_plane(plane_ref[0], functools.partial(add, (n,)))
        for t in targets:
            share_ref[t] = acc_ref[t].astype(BF)

    def staged():
        buf, sems = extra[1:]

        def copy(n, z):
            return pltpu.make_async_copy(block(n, z), buf.at[n], sems.at[n])

        def start(z):
            for n in range(4):
                copy(n, z).start()

        on_plane(plane_ref[0], start)
        for n in range(4):
            copy(n, 0).wait()
        acc_ref[...] = jnp.zeros_like(acc_ref)
        add((0, 1, 2, 3), 0, lambda n, z: buf.at[n])
        share_ref[...] = acc_ref[...].astype(BF)

    if part is None:
        run((0, 1, 2, 3))
        return

    @pl.when(core_ref[0] == 1)
    def _():
        if part == 0:
            run((0, 1, 2))
            extra[0][...] = acc_ref[...]
        else:
            finish(3)

    if part == 1:

        @pl.when(core_ref[0] == 0)
        def _():
            staged()


STAGE = [pltpu.VMEM((4, PACKED, WIDTH, WIDTH), BF), pltpu.SemaphoreType.DMA((4,))]
NODE_F32 = jax.ShapeDtypeStruct((4, COLS, WIDTH), F32)
NODE_BF = jax.ShapeDtypeStruct((4, COLS, WIDTH), BF)
COPIES = jax.ShapeDtypeStruct((CHIPS, 4, COLS, WIDTH), BF)


def pick(level, factors):
    return [factors[r][k] for r in range(2) for k in used(level)]


def forward_part(level, part, here, at, gots, before, told, blocks):
    shares = jax.ShapeDtypeStruct((NODES, COLS, WIDTH), BF)
    out_shape = (NODE_F32, NODE_BF, shares)
    if part == 0:
        out_shape += (jax.ShapeDtypeStruct((NODES, COLS, WIDTH), F32),)
    return pl.pallas_call(
        functools.partial(forward_kernel, level, part),
        in_specs=[SMEM] * 3 + [VM] * (len(gots) + len(before) + 2 + len(blocks)),
        out_specs=(VM,) * len(out_shape),
        scratch_shapes=[pltpu.VMEM((NODES, COLS, WIDTH), F32)] + (STAGE if part == 1 else []),
        out_shape=out_shape,
        input_output_aliases={3 + len(gots) + 2: 2} if part == 1 else {},
        compiler_params=pltpu.CompilerParams(vmem_limit_bytes=LIMIT),
        cost_estimate=pl.CostEstimate(flops=2 * 36 * COLS * WIDTH**2, bytes_accessed=6 * MIB, transcendentals=0),
    )(*here, at, *gots, *before, *told, *blocks)


def forward_level(level, here, at, gots, told, factors):
    return forward_part(level, None, here, at, gots, (), told, pick(level, factors))


def forward_halves(level, here, at, gots, told, factors):
    early = [factors[0][k] for k in used(level)] + [factors[1][k] for k in used(level) if k < 6]
    before = forward_part(level, 0, here, at, gots, (), told, early)
    return forward_part(level, 1, here, at, gots, before, told, pick(level, factors))


def top_kernel(plane_ref, got_ref, own_told, other_told, *rest):
    refs, (fb_ref, sol_ref, copies_ref) = rest[:-3], rest[-3:]
    names = used(3)
    came = told_by(plane_ref[0], 3)
    resids = []
    for n in range(4):
        inflow = jnp.sum(got_ref[:, n].astype(F32), axis=0)
        resids.append((rows_of((own_told, other_told), came, n).astype(F32) - inflow).astype(BF))

    def run(z):
        invs = [refs[len(names) * (n // 2) + names.index(WHERE[3][n % 2][z])].at[FAN] for n in range(4)]
        solved = []
        for n in range(4):
            solved.append(dot_t(resids[n], invs[n][...]).astype(BF))
            fb_ref[n] = solved[n]
        for n in range(4):
            sol = dot_n(solved[n], invs[n][...]).astype(BF)
            sol_ref[n] = sol
            for k in range(CHIPS):
                copies_ref[k, n] = sol

    on_plane(plane_ref[0], run)


def top_level(plane, got, told, factors):
    blocks = pick(3, factors)
    return pl.pallas_call(
        top_kernel,
        in_specs=[SMEM] + [VM] * (3 + len(blocks)),
        out_specs=(VM, VM, VM),
        out_shape=(NODE_BF, NODE_BF, COPIES),
        compiler_params=pltpu.CompilerParams(vmem_limit_bytes=LIMIT),
        cost_estimate=pl.CostEstimate(flops=2 * 8 * COLS * WIDTH**2, bytes_accessed=3 * MIB, transcendentals=0),
    )(plane, got, *told, *blocks)


def backward_kernel(level, plane_ref, at_ref, above_ref, f_ref, *rest):
    names = used(level)
    refs, outs = rest[: 2 * len(names)], rest[2 * len(names) :]
    came = told_by(plane_ref[0], level)

    def run(z):
        blocks = [refs[len(names) * (n // 2) + names.index(WHERE[level][n % 2][z])] for n in range(4)]
        uppers = []
        for n in range(4):
            picked = jnp.concatenate([above_ref[at_ref[came, n, p]] for p in range(FAN)], axis=1)
            back = dot_n(picked, blocks[n][:FAN].reshape(FAN * WIDTH, WIDTH))
            uppers.append((f_ref[n] - back).astype(BF))
        for n in range(4):
            sol = dot_n(uppers[n], blocks[n][FAN]).astype(BF)
            outs[0][n] = sol
            if level:
                for k in range(CHIPS):
                    outs[1][k, n] = sol

    on_plane(plane_ref[0], run)


def backward_level(level, plane, at, above, f, factors):
    blocks = pick(level, factors)
    out_shape = (NODE_BF, COPIES) if level else (NODE_BF,)
    return pl.pallas_call(
        functools.partial(backward_kernel, level),
        in_specs=[SMEM, SMEM] + [VM] * (2 + len(blocks)),
        out_specs=(VM,) * len(out_shape),
        out_shape=out_shape,
        compiler_params=pltpu.CompilerParams(vmem_limit_bytes=LIMIT),
        cost_estimate=pl.CostEstimate(flops=2 * 36 * COLS * WIDTH**2, bytes_accessed=6 * MIB, transcendentals=0),
    )(plane, at, above, f, *blocks)


def last_kernel(core_ref, own_ref, other_ref, forward_ref, result_ref):
    core = core_ref[0]
    for k, out_ref in enumerate((forward_ref, result_ref)):
        for j in range(2):
            own = jnp.concatenate([own_ref[z, k, 0, j] for z in range(4)], axis=0).astype(F32)
            other = jnp.concatenate([other_ref[z, k, 1, j] for z in range(4)], axis=0).astype(F32)
            low, high = jnp.where(core == 0, own, other), jnp.where(core == 0, other, own)
            out_ref[j] = jnp.transpose(jnp.concatenate([low, high], axis=0))


def last_step(core, own, other):
    return pl.pallas_call(
        last_kernel,
        out_shape=(jax.ShapeDtypeStruct((2, WIDTH, WIDTH), F32),) * 2,
        in_specs=[SMEM, VM, VM],
        out_specs=(VM, VM),
        compiler_params=pltpu.CompilerParams(vmem_limit_bytes=8 * MIB),
        cost_estimate=pl.CostEstimate(flops=0, bytes_accessed=2 * MIB, transcendentals=0),
    )(core, own, other)


def swap(value):
    return lax.ppermute(value, "c", [(0, 1), (1, 0)])


def exchange(value):
    return lax.all_to_all(value.reshape(CHIPS, 4, COLS, WIDTH), ("y", "x"), 0, 0, tiled=True)


def on_device(rhs, inverses, blocks, pattern):
    core = lax.axis_index("c").astype(jnp.int32)
    plane = lax.axis_index("z").astype(jnp.int32)
    core1, plane1 = core.reshape(1), plane.reshape(1)
    factor = blocks.reshape(2, FAN, WIDTH, WIDTH)
    inverse = inverses.reshape(2, WIDTH, WIDTH)

    with jax.named_scope("tell_planes"):
        message = pack(core1, plane1, pattern.reshape(2, FAN), rhs.reshape(2, WIDTH, WIDTH))
        told = [message[0]]
        for k in range(1, 4):
            told.append(lax.ppermute(message[k], "z", [(z, (z + k) % 4) for z in range(4)]))

    with jax.named_scope("factor_step_1"):
        own_a, own_b = join(0, factor, inverse), join(1, factor, inverse)
        own_a, own_b, told = lax.optimization_barrier((own_a, own_b, told))
        up_1 = lax.ppermute(own_a, "z", UP)
        down_1 = lax.ppermute(own_b, "z", DOWN)
        near_a, near_b = swap(own_a), swap(own_b)

    with jax.named_scope("tell_planes"):
        told = jnp.stack(told)
        told = (told, swap(told))
        targets = jnp.concatenate([t[:, PAT : PAT + 2, :FAN] for t in told], axis=1).astype(jnp.int32)
        targets = jnp.clip(targets, 0, NODES - 1)
        chip = targets % 8 // 2 * 4 + targets % 32 // 8
        places = chip * 4 + jnp.bitwise_xor(targets % 2, core) * 2 + targets // 32

    with jax.named_scope("factor_step_2"):
        up_2 = lax.ppermute(choose(plane1, 0, own_b, up_1), "z", UP)
        down_2 = lax.ppermute(choose(plane1, 3, down_1, own_a), "z", DOWN)
        up_3 = choose(plane1, 0, up_1, own_b)
        down_3 = choose(plane1, 3, own_a, down_1)
        near = (near_a, near_b, swap(up_1), swap(down_1))
        up_2, down_2, up_3, down_3, told, places, near = lax.optimization_barrier(
            (up_2, down_2, up_3, down_3, told, places, near)
        )
        near += (swap(up_2), swap(down_2))
    with jax.named_scope("factor_step_3"):
        up_3 = lax.ppermute(up_3, "z", UP)
        down_3 = lax.ppermute(down_3, "z", DOWN)

    factors = ([own_a, own_b, up_1, down_1, up_2, down_2], list(near))
    forward = [None] * 3
    solved = [None] * 4
    gots = ()
    for level in range(3):
        with jax.named_scope(f"forward_{level}"):
            solve = forward_halves if level == 1 else forward_level
            forward[level], solved[level], share = solve(level, (core1, plane1), places, gots, told, factors)
            got = exchange(share)
        if level == 0:
            with jax.named_scope("factor_step_3"):
                up_3, down_3, got = lax.optimization_barrier((up_3, down_3, inflow_of(got)))
                factors[0].extend([up_3, down_3])
                factors[1].extend([swap(up_3), swap(down_3)])
        gots = (got,)
    result = [None] * 4
    with jax.named_scope("top"):
        solved[3], result[3], copies = top_level(plane1, got, told, factors)

    for level in (2, 1, 0):
        with jax.named_scope(f"backward_{level}"):
            above = exchange(copies).reshape(NODES, COLS, WIDTH)
            out = backward_level(level, plane1, places, above, forward[level], factors)
            result[level] = out[0]
            if level > 0:
                copies = out[1]

    with jax.named_scope("to_planes"):
        fx = jnp.stack([jnp.stack(solved), jnp.stack(result)], axis=1).reshape(4, 2, 2, 2, COLS, WIDTH)
        fx = lax.all_to_all(fx, "z", 0, 0, tiled=True)
        forward_out, result_out = last_step(core1, fx, swap(fx))
    shape = (1, 2, 1, WIDTH, WIDTH)
    return forward_out.reshape(shape), result_out.reshape(shape)


def solution(mesh):
    wide = Mesh(mesh.devices.reshape(4, 4, 2, 4), ("x", "y", "c", "z"))
    blk = ("x", "y", "c")
    return jax.shard_map(
        on_device,
        mesh=wide,
        in_specs=(
            P("z", None, blk, None, None),
            P("z", None, blk, None, None),
            P("z", None, blk, None, None, None),
            P("z", None, blk, None),
        ),
        out_specs=(P("z", None, blk, None, None), P("z", None, blk, None, None)),
        check_vma=False,
    )
```
